128 devices in a mesh: section: 2 (over core), replica: 32 (over z, y, x_lo), tensor: 2 (over x_hi).
Axes of the slice: x: 4 (x_hi: 2, x_lo: 2; x = x_hi * 2 + x_lo), y: 4, z: 4, core: 2. Of those that a mesh axis runs over, the one named last changes fastest.
Arguments:
- source_slot: int32 [192], replicated, may hold values from 0 to 191, as said below
- lengths: int32 [192], replicated, may hold values from 1 to 1280, as said below
- block_table: int32 [192, 80], P('replica'), may hold values from 0 to 479, as said below
- queries: bfloat16 [2, 192, 8192], P('section', 'replica', 'tensor'), may hold values from -32 to 32
- kv_pool: bfloat16 [2, 2, 15360, 16, 1024], P('section', None, 'replica', None, 'tensor'), may hold values from -8 to 8
- new_kv: bfloat16 [2, 2, 192, 1024], P('section', None, 'replica', 'tensor'), may hold values from -8 to 8
- ssm_state: float32 [2, 192, 16, 16384], P('section', 'replica', None, 'tensor'), may hold values from -6 to 6
- conv_out: bfloat16 [2, 192, 16384], P('section', 'replica', 'tensor'), may hold values from -6 to 6
- dt_raw: bfloat16 [2, 192, 16384], P('section', 'replica', 'tensor'), may hold values from -6 to 6
- x_proj: bfloat16 [2, 32, 16384], P('section', None, 'tensor'), may hold values from -0.046875 to 0.046875
- a_log: float32 [2, 16, 16384], P('section', None, 'tensor'), may hold values from -3 to 1.5
- dt_bias: float32 [2, 16384], P('section', 'tensor'), may hold values from -4 to 0
- skip_gain: float32 [2, 16384], P('section', 'tensor'), may hold values from 0.5 to 1.5
Outputs:
- handed_mamba: bfloat16 [2, 192, 16384], P('section', 'replica', 'tensor')
- handed_attention: bfloat16 [2, 192, 8192], P('section', 'replica', 'tensor')
- new_state: float32 [2, 192, 16, 16384], P('section', 'replica', None, 'tensor')
The draws below stay inside these ranges and needn't reach their ends.
Inputs may be any that keep to these rules, and one draw needn't show every extreme that they name: `source_slot`: slot g belongs to replica g // 6; the entries form a permutation of the slots; for every bit b below 5, each replica gives exactly one request to the replica whose index differs from its own in bit b and takes exactly one request from it; the other slots keep their requests. `lengths`: some slot holds exactly 1280 tokens. `block_table`: the rows of one replica's 6 slots together name each of its pages once.
All inputs are finite; a program needn't handle non-finite values.
Results may differ from the reference program's by a relative error of at most 0.0055.
Values may be sent and summed in bfloat16 or wider, within the bound.
No kernel may reach another device: no remote copies, remote signals or barrier semaphores. Data moves between devices by JAX's collectives and lax.ppermute only.
A program may use at most 192 MiB of HBM per device.

```python
import jax
import jax.numpy as jnp
from jax import lax

HEADS = 64
KVH = 8
HD = 128
DI = 16384
NSTATE = 16
PAGE = 16
SLOTS = 6
MAXP = 80
REPLICAS = 32
SECTIONS = 2
MOVES = 5
REQS = 192
POOL = 480
POOLS = 15360
LMAX = 1280


def draw_source_slot(key, part):
    key = jax.random.fold_in(key, 11)
    orders = jax.vmap(lambda index_value: jax.random.permutation(jax.random.fold_in(key, index_value), SLOTS))(jnp.arange(REPLICAS)).astype(jnp.int32)
    replica_ids = jnp.broadcast_to(jnp.arange(REPLICAS, dtype=jnp.int32)[:, None], (REPLICAS, SLOTS))
    rank_ids = jnp.broadcast_to(jnp.arange(SLOTS, dtype=jnp.int32)[None, :], (REPLICAS, SLOTS))
    flips = jnp.where(rank_ids < MOVES, jnp.left_shift(jnp.ones_like(rank_ids), jnp.minimum(rank_ids, 30)), 0).astype(jnp.int32)
    from_replica = jnp.bitwise_xor(replica_ids, flips)
    from_slot = orders[from_replica, rank_ids]
    destination = replica_ids * SLOTS + orders
    anchor_slot = from_replica * SLOTS + from_slot
    return jnp.zeros((REQS,), jnp.int32).at[destination.reshape(-1)].set(anchor_slot.reshape(-1))


def draw_lengths(key, part):
    key = jax.random.fold_in(key, 12)
    count_key, pick_key = jax.random.split(key)
    drawn = jax.random.randint(count_key, (REQS,), 1, LMAX + 1, jnp.int32)
    chosen = jax.random.randint(pick_key, (), 0, REQS, jnp.int32)
    return drawn.at[chosen].set(LMAX)


def draw_block_table(key, part):
    key = jax.random.fold_in(key, 13)
    pages = jax.vmap(lambda index_value: jax.random.permutation(jax.random.fold_in(key, index_value), POOL))(jnp.arange(REPLICAS))
    return pages.reshape(REQS, MAXP).astype(jnp.int32)


def draw_queries(key, part):
    key = jax.random.fold_in(key, 5)
    noise_key = jax.random.fold_in(key, 0)
    full_shape = (SECTIONS, REQS, HEADS, HD)
    drawn = jax.random.truncated_normal(noise_key, -6.0, 6.0, full_shape, jnp.float32)
    return drawn.reshape(SECTIONS, REQS, HEADS * HD).astype(jnp.bfloat16)


def draw_kv_pool(key, part):
    key = jax.random.fold_in(key, 3)
    noise_key = jax.random.fold_in(key, 0)
    full_shape = (SECTIONS, 2, POOLS, PAGE, KVH, HD)
    drawn = jax.random.truncated_normal(noise_key, -6.0, 6.0, full_shape, jnp.float32)
    return drawn.reshape(SECTIONS, 2, POOLS, PAGE, KVH * HD).astype(jnp.bfloat16)


def draw_new_kv(key, part):
    key = jax.random.fold_in(key, 4)
    noise_key = jax.random.fold_in(key, 0)
    full_shape = (SECTIONS, 2, REQS, KVH, HD)
    drawn = jax.random.truncated_normal(noise_key, -6.0, 6.0, full_shape, jnp.float32)
    return drawn.reshape(SECTIONS, 2, REQS, KVH * HD).astype(jnp.bfloat16)


def shard_levels(stream_key, dims, shards, least, largest):
    def one(dim, shards_of):
        steps = jax.random.uniform(jax.random.fold_in(jax.random.fold_in(stream_key, 6), dim), (shards_of,), jnp.float32, least / len(shards), largest / len(shards))
        return jnp.repeat(jnp.exp(steps), dims[dim] // shards_of).reshape((-1,) + (1,) * (len(dims) - dim - 1))

    factor_of = one(*shards[0])
    for cut in shards[1:]:
        factor_of = factor_of * one(*cut)
    return factor_of


def centred(stream_key, extent, scale, limit, cuts=(), kind=jnp.bfloat16):
    factor_of = shard_levels(stream_key, extent, cuts, -0.22, 0.18) if cuts else 1.0
    values = jax.random.normal(stream_key, extent, jnp.float32) * scale * factor_of
    return jnp.minimum(jnp.maximum(values, -limit), limit).astype(kind)


def setup_inputs(seed: int = 0) -> dict:
    key_list = jax.random.split(jax.random.key(seed), 14)
    source_slot = draw_source_slot(jax.random.fold_in(key_list[13], 71), 0)
    lengths = draw_lengths(jax.random.fold_in(key_list[13], 71), 0)
    block_table = draw_block_table(jax.random.fold_in(key_list[13], 71), 0)
    queries = draw_queries(jax.random.fold_in(key_list[13], 71), 0)
    kv_pool = draw_kv_pool(jax.random.fold_in(key_list[13], 71), 0)
    new_kv = draw_new_kv(jax.random.fold_in(key_list[13], 71), 0)
    ssm_state = centred(key_list[6], (SECTIONS, REQS, NSTATE, DI), 1.0, 6.0, ((0, 2), (1, 32), (3, 2)), jnp.float32)
    conv_out = centred(key_list[7], (SECTIONS, REQS, DI), 1.0, 6.0, ((0, 2), (1, 32), (2, 2)))
    dt_raw = centred(key_list[8], (SECTIONS, REQS, DI), 1.0, 6.0, ((0, 2), (1, 32), (2, 2)))
    x_proj = centred(key_list[9], (SECTIONS, 2 * NSTATE, DI), DI ** -0.5, 0.046875, ((0, 2), (2, 2)))
    a_log = jnp.clip(-3.0 + 4.5 * jax.random.uniform(key_list[10], (SECTIONS, NSTATE, DI), jnp.float32) ** shard_levels(key_list[10], (SECTIONS, NSTATE, DI), ((0, 2), (2, 2)), -0.2, 0.2), -3.0, 1.5)
    dt_bias = jnp.clip(-4.0 + 4.0 * jax.random.uniform(key_list[11], (SECTIONS, DI), jnp.float32) ** shard_levels(key_list[11], (SECTIONS, DI), ((0, 2), (1, 2)), -0.2, 0.2), -4.0, 0.0)
    skip_gain = jnp.clip(1.0 + 0.1 * jax.random.normal(key_list[12], (SECTIONS, DI), jnp.float32), 0.5, 1.5)
    return dict(source_slot=source_slot, lengths=lengths, block_table=block_table, queries=queries, kv_pool=kv_pool, new_kv=new_kv, ssm_state=ssm_state, conv_out=conv_out, dt_raw=dt_raw, x_proj=x_proj, a_log=a_log, dt_bias=dt_bias, skip_gain=skip_gain)


masked_score = -1.0e30


def segment_step(segment_items, source_slot, page_index, live_mask):
    query_rows, pool_rows, fresh_rows, state_rows, mixer_in, dt_input, x_weight, log_rates, bias_dt, skip_weight = segment_items
    previous = state_rows[source_slot]
    step_size = jax.nn.softplus(dt_input.astype(jnp.float32) + bias_dt)
    coupled = jnp.dot(mixer_in, x_weight.T, preferred_element_type=jnp.float32)
    input_gain = coupled[:, :NSTATE]
    read_gain = coupled[:, NSTATE:]
    mixer_float = mixer_in.astype(jnp.float32)
    decay_rate = jnp.exp(-step_size[:, None, :] * jnp.exp(log_rates)[None, :, :])
    updated = decay_rate * previous + (step_size * mixer_float)[:, None, :] * input_gain[:, :, None]
    mixed_rows = (jnp.sum(read_gain[:, :, None] * updated, axis=1) + skip_weight * mixer_float).astype(jnp.bfloat16)
    group_size = HEADS // KVH
    score_scale = HD ** -0.5
    key_rows = pool_rows[0][page_index].reshape(REQS, LMAX, KVH, HD).astype(jnp.float32)
    value_rows = pool_rows[1][page_index].reshape(REQS, LMAX, KVH, HD).astype(jnp.float32)
    head_rows = query_rows.reshape(REQS, KVH, group_size, HD).astype(jnp.float32)
    scores = jnp.einsum("rkgd,rtkd->rkgt", head_rows, key_rows) * score_scale
    allowed = live_mask[:, None, None, :]
    masked = jnp.where(allowed, scores, masked_score)
    cache_peak = jnp.max(masked, axis=-1)
    weights = jnp.where(allowed, jnp.exp(masked - cache_peak[..., None]), 0.0)
    cache_total = jnp.sum(weights, axis=-1)
    rounded = lax.optimization_barrier(weights.astype(jnp.bfloat16))
    gathered = jnp.einsum("rkgt,rtkd->rkgd", rounded.astype(jnp.float32), value_rows)
    own_keys = fresh_rows[0].reshape(REQS, KVH, HD).astype(jnp.float32)
    own_values = fresh_rows[1].reshape(REQS, KVH, HD).astype(jnp.float32)
    own_score = jnp.einsum("rkgd,rkd->rkg", head_rows, own_keys) * score_scale
    joint_peak = jnp.maximum(cache_peak, own_score)
    cache_weight = jnp.exp(cache_peak - joint_peak)
    own_weight = jnp.exp(own_score - joint_peak)
    numerator = cache_weight[..., None] * gathered + own_weight[..., None] * own_values[:, :, None, :]
    attended = numerator / (cache_weight * cache_total + own_weight)[..., None]
    attended = attended.reshape(REQS, HEADS * HD).astype(jnp.bfloat16)
    return mixed_rows, attended, updated


def reference(source_slot, lengths, block_table, queries, kv_pool, new_kv, ssm_state, conv_out, dt_raw, x_proj, a_log, dt_bias, skip_gain):
    anchor = (source_slot // SLOTS).astype(jnp.int32)
    page_index = (block_table[source_slot] + (anchor * POOL)[:, None]).astype(jnp.int32)
    live_mask = jnp.arange(LMAX, dtype=jnp.int32)[None, :] < lengths[:, None]

    def apply_segment(segment_items):
        return segment_step(segment_items, source_slot, page_index, live_mask)

    mixed_rows, attended, updated = lax.map(apply_segment, (queries, kv_pool, new_kv, ssm_state, conv_out, dt_raw, x_proj, a_log, dt_bias, skip_gain))
    return jnp.roll(mixed_rows, 1, axis=0), jnp.roll(attended, 1, axis=0), updated
```

```python
import jax
import jax.numpy as jnp
from jax import lax
from jax.experimental import pallas as pl
from jax.experimental.pallas import tpu as pltpu
from jax.sharding import PartitionSpec as P

HEADS = 64
KVH = 8
HD = 128

SLOTS = 6
BITS = 5
SEND_ORDER = (4, 2, 0, 3, 1)
BLOCK = 256

masked_score = -1e30
f32 = jnp.float32
bf16 = jnp.bfloat16


def swapped(value, axis, bit):
    mask = 2**bit
    pairs = [(source, source ^ mask) for source in range(lax.axis_size(axis))]
    return lax.ppermute(value, axis, pairs)


def across(value, bit):
    sections, replicas = lax.axis_size("section"), lax.axis_size("replica")
    mask = 0 if bit is None else 2**bit
    pairs = [
        (s * replicas + r, ((s + 1) % sections) * replicas + (r ^ mask))
        for s in range(sections)
        for r in range(replicas)
    ]
    return lax.ppermute(value, ("section", "replica"), pairs)


def whole(space):
    return pl.BlockSpec(memory_space=space)


def write_plan(own, src, lens, plan):
    first = own * SLOTS
    for entry in range(24):
        plan[entry] = 0
    for bit in range(BITS):
        partner = jnp.bitwise_xor(own, 1 << bit) * SLOTS
        leave = jnp.int32(0)
        served = jnp.int32(1)
        ask = jnp.int32(0)
        for j in range(SLOTS):
            there = src[partner + j] - first
            gives = (there >= 0) & (there < SLOTS)
            leave = jnp.where(gives, there, leave)
            served = jnp.where(gives, lens[partner + j], served)
            here = src[first + j] - partner
            ask = jnp.where((here >= 0) & (here < SLOTS), j, ask)
        plan[bit] = leave
        plan[8 + bit] = ask
        plan[16 + bit] = served
    kept_old = jnp.int32(0)
    kept_new = jnp.int32(0)
    for j in range(SLOTS):
        here = src[first + j] - first
        stays = (here >= 0) & (here < SLOTS)
        kept_old = jnp.where(stays, here, kept_old)
        kept_new = jnp.where(stays, j, kept_new)
    plan[5] = kept_old
    plan[13] = kept_new
    plan[21] = lens[first + kept_new]


def pack_kernel(
    src, lens, state, queries, fresh, conv, x_proj,
    plan, gains, kept, p0, p1, p2, p3, p4,
    state_buf, q_buf, fresh_buf, conv_buf, x_buf, head_rows, own_rows, sems,
):
    packs = (p0, p1, p2, p3, p4)
    width = state.shape[-1]
    small = [
        pltpu.make_async_copy(queries, q_buf, sems.at[5]),
        pltpu.make_async_copy(fresh, fresh_buf, sems.at[6]),
        pltpu.make_async_copy(conv, conv_buf, sems.at[7]),
        pltpu.make_async_copy(x_proj, x_buf, sems.at[8]),
    ]
    write_plan(lax.axis_index("replica"), src, lens, plan)
    copies = {}
    for bit in SEND_ORDER:
        copies[bit] = pltpu.make_async_copy(state.at[plan[bit]], state_buf.at[bit], sems.at[bit])
        copies[bit].start()
    for copy in small:
        copy.start()
    for copy in small:
        copy.wait()
    gains[...] = lax.dot_general(
        x_buf[...], conv_buf[...], (((1,), (1,)), ((), ())), preferred_element_type=f32
    )
    own_rows[...] = jnp.zeros_like(own_rows)
    heads = head_rows.shape[1]
    keys = fresh_buf.shape[-1] // HD
    for h in range(heads):
        column = q_buf[:, h * HD : (h + 1) * HD].astype(f32)
        for slot in range(SLOTS):
            head_rows[slot, h : h + 1, :] = column[slot : slot + 1]

    def heads_of(slot):
        pair = fresh_buf[slot].astype(f32)
        for k in range(keys):
            own_rows[k : k + 1, :] = pair[0:1, k * HD : (k + 1) * HD]
            own_rows[keys + k : keys + k + 1, :] = pair[1:2, k * HD : (k + 1) * HD]
        half = heads // 2
        return jnp.concatenate(
            [head_rows[slot, 0:half], head_rows[slot, half:heads], own_rows[...]], axis=1
        ).astype(bf16)

    for bit in SEND_ORDER:
        packs[bit][:, width:] = heads_of(plan[8 + bit])
        copies[bit].wait()
        packs[bit][:, :width] = state_buf[bit].astype(bf16)
    kept[...] = heads_of(plan[13])


def pack(source_slot, lengths, states, queries, fresh, conv, x_proj):
    n, width = states.shape[1:]
    heads = queries.shape[1] // HD
    half = heads // 2
    packed = jax.ShapeDtypeStruct((half, width + 3 * HD), bf16)
    return pl.pallas_call(
        pack_kernel,
        out_shape=(
            jax.ShapeDtypeStruct((24,), jnp.int32),
            pltpu.VMEM((x_proj.shape[0], SLOTS), f32),
            pltpu.VMEM((half, 3 * HD), bf16),
        )
        + (pltpu.VMEM(packed.shape, bf16),) * BITS,
        in_specs=[whole(pltpu.SMEM)] * 2 + [whole(pl.ANY)] * 5,
        out_specs=(whole(pltpu.SMEM),) + (whole(pltpu.VMEM),) * (2 + BITS),
        scratch_shapes=[
            pltpu.VMEM((BITS, n, width), f32),
            pltpu.VMEM(queries.shape, bf16),
            pltpu.VMEM(fresh.shape, bf16),
            pltpu.VMEM(conv.shape, bf16),
            pltpu.VMEM(x_proj.shape, bf16),
            pltpu.VMEM((SLOTS, heads, HD), f32),
            pltpu.VMEM((half, HD), f32),
            pltpu.SemaphoreType.DMA((9,)),
        ],
        compiler_params=pltpu.CompilerParams(vmem_limit_bytes=24 * 2**20),
        cost_estimate=pl.CostEstimate(
            flops=2 * 32 * 8 * width, transcendentals=0, bytes_accessed=5 * n * width * 6
        ),
    )(source_slot, lengths, states, queries, fresh, conv, x_proj)


def attend_kernel(items, plan, table, pool, *refs):
    extras, outs = refs[: len(items)], refs[len(items) :]
    page = pool.shape[2]
    pages = table.shape[1]
    tokens = page * pages
    per_block = BLOCK // page
    blocks = pages // per_block
    width = pool.shape[3]
    pair_width = 2 * HD
    pairs = width // pair_width
    group = HEADS // KVH
    rows = 2 * group
    scale = HD ** (-0.5)
    row_id = lax.broadcasted_iota(jnp.int32, (rows, pair_width), 0)
    lane_id = lax.broadcasted_iota(jnp.int32, (rows, pair_width), 1)
    own_block = (row_id < group) == (lane_id < HD)
    token_id = lax.broadcasted_iota(jnp.int32, (rows * pairs, BLOCK), 1)
    for item, extra, out in zip(items, extras, outs):
        slot = plan[item]
        length = plan[16 + item]
        base = extra.shape[1] - 3 * HD
        halves = [extra[:, base + i * HD : base + (i + 1) * HD].astype(f32) for i in range(2)]
        own = extra[:, base + 2 * HD :].astype(f32)
        spread = [
            jnp.where(own_block, jnp.concatenate([half, half], axis=1), 0.0).astype(bf16)
            for half in halves
        ]
        places = [table[slot, p] for p in range(pages)]

        def block_of(which, j):
            return jnp.concatenate(
                [pool[which, places[j * per_block + u]] for u in range(per_block)], axis=0
            )

        scores = []
        for j in range(blocks):
            keys = block_of(0, j)
            parts = [
                lax.dot_general(
                    spread[i],
                    keys[:, i * pair_width : (i + 1) * pair_width],
                    (((1,), (1,)), ((), ())),
                    preferred_element_type=f32,
                )
                for i in range(pairs)
            ]
            score = jnp.concatenate(parts, axis=0) * scale
            scores.append(jnp.where(token_id < length - j * BLOCK, score, masked_score))
        top = scores[0]
        for score in scores[1:]:
            top = jnp.maximum(top, score)
        cache_peak = jnp.max(top, axis=1, keepdims=True)
        weights = [jnp.exp(score - cache_peak) for score in scores]
        summed = weights[0]
        for weight in weights[1:]:
            summed = summed + weight
        cache_total = jnp.sum(summed, axis=1, keepdims=True)
        full = [None] * pairs
        for j in range(blocks):
            values = block_of(1, j)
            rounded = weights[j].astype(bf16)
            for i in range(pairs):
                part = jnp.dot(
                    rounded[i * rows : (i + 1) * rows],
                    values[:, i * pair_width : (i + 1) * pair_width],
                    preferred_element_type=f32,
                )
                full[i] = part if full[i] is None else full[i] + part
        gathered = jnp.concatenate(
            [
                full[k // 2][(k % 2) * group : (k % 2 + 1) * group, (k % 2) * HD : (k % 2 + 1) * HD]
                for k in range(2 * pairs)
            ],
            axis=0,
        )
        kv_heads = 2 * pairs
        own_keys = jnp.concatenate(
            [jnp.broadcast_to(own[k : k + 1], (group, HD)) for k in range(kv_heads)], axis=0
        )
        own_values = jnp.concatenate(
            [jnp.broadcast_to(own[kv_heads + k : kv_heads + k + 1], (group, HD)) for k in range(kv_heads)],
            axis=0,
        )
        head_rows = jnp.concatenate(halves, axis=0)
        own_score = jnp.sum(head_rows * own_keys, axis=1, keepdims=True) * scale
        joint_peak = jnp.maximum(cache_peak, own_score)
        cache_weight = jnp.exp(cache_peak - joint_peak)
        own_weight = jnp.exp(own_score - joint_peak)
        numerator = cache_weight * gathered + own_weight * own_values
        attended = numerator / (cache_weight * cache_total + own_weight)
        out[...] = attended.astype(bf16)


def attend(items, plan, table, pool, extras):
    heads = pool.shape[-1] // HD * (HEADS // KVH)
    pool = pltpu.with_memory_space_constraint(pool, pltpu.VMEM)
    extras = [pltpu.with_memory_space_constraint(extra, pltpu.VMEM) for extra in extras]

    def kernel(*refs):
        attend_kernel(items, *refs)

    return pl.pallas_call(
        kernel,
        out_shape=(pltpu.VMEM((heads, HD), bf16),) * len(items),
        in_specs=[whole(pltpu.SMEM)] * 2 + [whole(pltpu.VMEM)] * (1 + len(items)),
        out_specs=(whole(pltpu.VMEM),) * len(items),
        compiler_params=pltpu.CompilerParams(vmem_limit_bytes=16 * 2**20),
        cost_estimate=pl.CostEstimate(
            flops=len(items) * 4 * 1280 * 32 * 512,
            transcendentals=len(items) * 1280 * 32,
            bytes_accessed=len(items) * 2 * 80 * 16 * 1024,
        ),
    )(plan, table, pool, *extras)


def update_kernel(
    plan, gains, gains_far, state, conv, dt, a_log, bias, skip, r0, r1, r2, r3, r4,
    new_state, mixed,
    state_buf, a_buf, rate, step_rows, drive_rows, mixer_rows, mixed_rows, out_buf, sems,
):
    moved = (r0, r1, r2, r3, r4)
    n, width = a_buf.shape
    states_in = pltpu.make_async_copy(state.at[plan[5]], state_buf, sems.at[6])
    states_in.start()
    rates_in = pltpu.make_async_copy(a_log, a_buf, sems.at[7])
    rates_in.start()
    mixer = conv[...].astype(f32)
    step_in = dt[...].astype(f32) + bias[...]
    step = jnp.maximum(step_in, 0.0) + jnp.log1p(jnp.exp(-jnp.abs(step_in)))
    drive = step * mixer
    mixer_rows[...] = skip[...] * mixer
    for row in range(SLOTS):
        step_rows[row] = step[row : row + 1]
        drive_rows[row] = drive[row : row + 1]
    coupled = gains[...] + gains_far[...]
    lane = lax.broadcasted_iota(jnp.int32, coupled.shape, 1)
    rates_in.wait()
    rate[...] = -jnp.exp(a_buf[...])
    outs = []
    chunk = 512
    for item in SEND_ORDER + (5,):
        slot = plan[8 + item]
        column = jnp.sum(jnp.where(lane == slot, coupled, 0.0), axis=1, keepdims=True)
        input_gain = jnp.broadcast_to(column[0:n], (n, 128))
        read_gain = jnp.broadcast_to(column[n : 2 * n], (n, 128))
        if item == 5:
            states_in.wait()
        target = out_buf.at[item]

        def body(c, _, item=item, slot=slot, input_gain=input_gain, read_gain=read_gain, target=target):
            for u in range(chunk // 128):
                at = pl.ds(pl.multiple_of(c * chunk + u * 128, 128), 128)
                if item == 5:
                    previous = state_buf[:, at]
                else:
                    previous = moved[item][:, at].astype(f32)
                step_row = jnp.broadcast_to(step_rows[slot, :, at], (n, 128))
                drive_row = jnp.broadcast_to(drive_rows[slot, :, at], (n, 128))
                updated = jnp.exp(step_row * rate[:, at]) * previous + drive_row * input_gain
                target[:, at] = updated
                mixed_rows[slot, :, at] = jnp.sum(read_gain * updated, axis=0, keepdims=True)
            return 0

        lax.fori_loop(0, width // chunk, body, 0)
        copy = pltpu.make_async_copy(target, new_state.at[slot], sems.at[item])
        copy.start()
        outs.append(copy)
    for row in range(SLOTS):
        mixer_rows[row : row + 1, :] += mixed_rows[row]
    mixed[...] = mixer_rows[...].astype(bf16)
    for copy in outs:
        copy.wait()


def update(plan, gains, gains_far, states, conv, dt, a_log, bias, skip, moved):
    slots, n, width = states.shape
    moved = [pltpu.with_memory_space_constraint(value, pltpu.VMEM) for value in moved]
    rows = pltpu.VMEM((slots, 1, width), f32)
    return pl.pallas_call(
        update_kernel,
        out_shape=(
            jax.ShapeDtypeStruct(states.shape, f32),
            pltpu.VMEM(conv.shape, bf16),
        ),
        in_specs=[whole(pltpu.SMEM)]
        + [whole(pltpu.VMEM)] * 2
        + [whole(pl.ANY)]
        + [whole(pltpu.VMEM)] * 2
        + [whole(pl.ANY)]
        + [whole(pltpu.VMEM)] * (2 + BITS),
        out_specs=(whole(pl.ANY), whole(pltpu.VMEM)),
        scratch_shapes=[
            pltpu.VMEM((n, width), f32),
            pltpu.VMEM((n, width), f32),
            pltpu.VMEM((n, width), f32),
            rows,
            rows,
            pltpu.VMEM((slots, width), f32),
            rows,
            pltpu.VMEM((slots, n, width), f32),
            pltpu.SemaphoreType.DMA((8,)),
        ],
        compiler_params=pltpu.CompilerParams(vmem_limit_bytes=24 * 2**20),
        cost_estimate=pl.CostEstimate(
            flops=slots * n * width * 8,
            transcendentals=slots * n * width,
            bytes_accessed=slots * n * width * 6 + 2 * n * width * 4,
        ),
    )(plan, gains, gains_far, states, conv, dt, a_log, bias, skip, *moved)


def place_kernel(plan, a0, a1, a2, a3, a4, a5, out, head_rows, rows):
    for item, value in enumerate((a0, a1, a2, a3, a4, a5)):
        head_rows[plan[8 + item]] = value[...].astype(f32)
    for slot in range(SLOTS):
        for h in range(head_rows.shape[1]):
            rows[slot : slot + 1, h * HD : (h + 1) * HD] = head_rows[slot, h : h + 1, :]
    out[...] = rows[...].astype(bf16)


def place(plan, parts):
    heads = parts[0].shape[0]
    return pl.pallas_call(
        place_kernel,
        out_shape=jax.ShapeDtypeStruct((SLOTS, heads * HD), bf16),
        in_specs=[whole(pltpu.SMEM)] + [whole(pltpu.VMEM)] * (BITS + 1),
        out_specs=whole(pltpu.VMEM),
        scratch_shapes=[pltpu.VMEM((SLOTS, heads, HD), f32), pltpu.VMEM((SLOTS, heads * HD), f32)],
    )(plan, *parts)


def per_device(
    source_slot,
    lengths,
    block_table,
    queries,
    kv_pool,
    new_kv,
    ssm_state,
    conv_out,
    dt_raw,
    x_proj,
    a_log,
    dt_bias,
    skip_gain,
):
    fresh = jnp.transpose(new_kv[0], (1, 0, 2))
    plan, gains, kept, *packs = pack(
        source_slot, lengths, ssm_state[0], queries[0], fresh, conv_out[0], x_proj[0]
    )
    moved = [None] * BITS
    for bit in SEND_ORDER:
        moved[bit] = swapped(packs[bit], "replica", bit)
    gains_far = swapped(gains, "tensor", 0)
    items = SEND_ORDER + (5,)
    extras = [moved[bit] for bit in SEND_ORDER] + [kept]
    attended = attend(items, plan, block_table, kv_pool[0], extras)
    back = [None] * (BITS + 1)
    for item, value in zip(items, attended):
        back[item] = across(value, item if item < BITS else None)
    new_state, mixed = update(
        plan, gains, gains_far, ssm_state[0], conv_out[0], dt_raw[0], a_log[0], dt_bias, skip_gain, moved
    )
    handed_mamba = across(mixed, None)
    handed_attention = place(plan, back)
    return handed_mamba[None], handed_attention[None], new_state[None]


def solution(mesh):
    in_specs = (
        P(),
        P(),
        P("replica", None),
        P("section", "replica", "tensor"),
        P("section", None, "replica", None, "tensor"),
        P("section", None, "replica", "tensor"),
        P("section", "replica", None, "tensor"),
        P("section", "replica", "tensor"),
        P("section", "replica", "tensor"),
        P("section", None, "tensor"),
        P("section", None, "tensor"),
        P("section", "tensor"),
        P("section", "tensor"),
    )
    out_specs = (
        P("section", "replica", "tensor"),
        P("section", "replica", "tensor"),
        P("section", "replica", None, "tensor"),
    )
    return jax.shard_map(
        per_device, mesh=mesh, in_specs=in_specs, out_specs=out_specs, check_vma=False
    )
```

```python
import jax
import jax.numpy as jnp
from jax import lax
from jax.experimental import pallas as pl
from jax.experimental.pallas import tpu as pltpu
from jax.sharding import PartitionSpec as P

HEADS = 64
KVH = 8
HD = 128

SLOTS = 6
BITS = 5
SEND_ORDER = (4, 2, 0, 3, 1)
FIRST = (5, 4, 2)
LAST = (0, 3, 1)
BLOCK = 256
LOG2E = 1.4426950408889634
PACK_WEIGHT = 10000

masked_score = -1e30
f32 = jnp.float32
bf16 = jnp.bfloat16


def swapped(value, axis, bit):
    mask = 2**bit
    pairs = [(source, source ^ mask) for source in range(lax.axis_size(axis))]
    return lax.ppermute(value, axis, pairs)


def across(value, bit):
    sections, replicas = lax.axis_size("section"), lax.axis_size("replica")
    mask = 2**bit if bit < BITS else 0
    pairs = [
        (s * replicas + r, ((s + 1) % sections) * replicas + (r ^ mask))
        for s in range(sections)
        for r in range(replicas)
    ]
    return lax.ppermute(value, ("section", "replica"), pairs)


def whole(space):
    return pl.BlockSpec(memory_space=space)


def in_hbm(*values):
    return [pltpu.with_memory_space_constraint(value, pltpu.HBM) for value in values]


def in_vmem(*values):
    return [pltpu.with_memory_space_constraint(value, pltpu.VMEM) for value in values]


def write_plan(own, src, lens, plan):
    first = own * SLOTS
    for entry in range(24):
        plan[entry] = 0
    for bit in range(BITS):
        partner = jnp.bitwise_xor(own, 1 << bit) * SLOTS
        leave = jnp.int32(0)
        served = jnp.int32(1)
        ask = jnp.int32(0)
        for j in range(SLOTS):
            there = src[partner + j] - first
            gives = (there >= 0) & (there < SLOTS)
            leave = jnp.where(gives, there, leave)
            served = jnp.where(gives, lens[partner + j], served)
            here = src[first + j] - partner
            ask = jnp.where((here >= 0) & (here < SLOTS), j, ask)
        plan[bit] = leave
        plan[8 + bit] = ask
        plan[16 + bit] = served
    kept_old = jnp.int32(0)
    kept_new = jnp.int32(0)
    for j in range(SLOTS):
        here = src[first + j] - first
        stays = (here >= 0) & (here < SLOTS)
        kept_old = jnp.where(stays, here, kept_old)
        kept_new = jnp.where(stays, j, kept_new)
    plan[5] = kept_old
    plan[13] = kept_new
    plan[21] = lens[first + kept_new]


def load_kernel(
    src_in, lens_in, state, queries, fresh, plan, held, heads_out,
    src, lens, q_buf, fresh_buf, head_rows, own_rows, sems,
):
    copies = [
        pltpu.make_async_copy(source, target, sems.at[i])
        for i, (source, target) in enumerate(
            ((src_in, src), (lens_in, lens), (queries, q_buf), (fresh, fresh_buf), (state, held))
        )
    ]
    for copy in copies:
        copy.start()
    copies[0].wait()
    copies[1].wait()
    write_plan(lax.axis_index("replica"), src, lens, plan)
    copies[2].wait()
    copies[3].wait()
    heads = head_rows.shape[1]
    half = heads // 2
    keys = fresh_buf.shape[-1] // HD
    own_rows[...] = jnp.zeros_like(own_rows)
    for h in range(heads):
        column = q_buf[:, h * HD : (h + 1) * HD].astype(f32)
        for slot in range(SLOTS):
            head_rows[slot, h : h + 1, :] = column[slot : slot + 1]
    for item in range(BITS + 1):
        slot = plan[8 + item]
        pair = fresh_buf[slot].astype(f32)
        for k in range(keys):
            own_rows[k : k + 1, :] = pair[0:1, k * HD : (k + 1) * HD]
            own_rows[keys + k : keys + k + 1, :] = pair[1:2, k * HD : (k + 1) * HD]
        heads_out[item] = jnp.concatenate(
            [head_rows[slot, 0:half], head_rows[slot, half:heads], own_rows[...]], axis=1
        ).astype(bf16)
    copies[4].wait()


def load(source_slot, lengths, states, queries, fresh):
    heads = queries.shape[1] // HD
    half = heads // 2
    return pl.pallas_call(
        load_kernel,
        out_shape=(
            pltpu.SMEM((24,), jnp.int32),
            pltpu.VMEM(states.shape, f32),
            pltpu.VMEM((BITS + 1, half, 3 * HD), bf16),
        ),
        in_specs=[whole(pl.ANY)] * 5,
        out_specs=(whole(pltpu.SMEM), whole(pltpu.VMEM), whole(pltpu.VMEM)),
        scratch_shapes=[
            pltpu.SMEM(source_slot.shape, jnp.int32),
            pltpu.SMEM(lengths.shape, jnp.int32),
            pltpu.VMEM(queries.shape, bf16),
            pltpu.VMEM(fresh.shape, bf16),
            pltpu.VMEM((SLOTS, heads, HD), f32),
            pltpu.VMEM((half, HD), f32),
            pltpu.SemaphoreType.DMA((5,)),
        ],
        compiler_params=pltpu.CompilerParams(vmem_limit_bytes=4 * 2**20),
        cost_estimate=pl.CostEstimate(flops=0, transcendentals=0, bytes_accessed=states.size * 4),
    )(*in_hbm(source_slot, lengths, states, queries, fresh))


def pack_kernel(plan, held, heads, *packs):
    width = held.shape[-1]
    for bit, out in zip(SEND_ORDER, packs):
        out[:, :width] = held[plan[bit]].astype(bf16)
        out[:, width:] = heads[bit]


def pack(plan, held, heads):
    n, width = held.shape[1:]
    packs = pl.pallas_call(
        pack_kernel,
        out_shape=(pltpu.VMEM((n, width + heads.shape[-1]), bf16),) * BITS,
        in_specs=[whole(pltpu.SMEM)] + [whole(pltpu.VMEM)] * 2,
        out_specs=(whole(pltpu.VMEM),) * BITS,
        compiler_params=pltpu.CompilerParams(vmem_limit_bytes=4 * 2**20),
        cost_estimate=pl.CostEstimate(
            flops=PACK_WEIGHT * held.size, transcendentals=0, bytes_accessed=held.size * 6
        ),
    )(plan, *in_vmem(held, heads))
    return dict(zip(SEND_ORDER, packs))


def attend_kernel(items, arrived, plan, table, pool, *refs):
    refs = list(refs)
    extras = [refs.pop(0) for _ in items]
    backs = [refs.pop(0) for _ in arrived]
    later = refs.pop(0)
    outs = [refs.pop(0) for _ in items]
    for entry in range(24):
        later[entry] = plan[entry]
    if arrived:
        placed = refs.pop(0)
        placed[...] = jnp.zeros_like(placed)
        for item, back in zip(arrived, backs):
            placed[plan[8 + item]] = back[...].astype(f32)
    page = pool.shape[2]
    pages = table.shape[1]
    tokens = page * pages
    per_block = BLOCK // page
    blocks = pages // per_block
    width = pool.shape[3]
    pair_width = 2 * HD
    pairs = width // pair_width
    group = HEADS // KVH
    rows = 2 * group
    scale = HD ** (-0.5)
    row_id = lax.broadcasted_iota(jnp.int32, (rows, pair_width), 0)
    lane_id = lax.broadcasted_iota(jnp.int32, (rows, pair_width), 1)
    own_block = (row_id < group) == (lane_id < HD)
    token_id = lax.broadcasted_iota(jnp.int32, (rows * pairs, BLOCK), 1)
    for item, extra, out in zip(items, extras, outs):
        slot = plan[item]
        length = plan[16 + item]
        if item == BITS:
            extra = extra.at[BITS]
        base = extra.shape[1] - 3 * HD
        halves = [extra[:, base + i * HD : base + (i + 1) * HD].astype(f32) for i in range(2)]
        own = extra[:, base + 2 * HD :].astype(f32)
        spread = [
            jnp.where(own_block, jnp.concatenate([half, half], axis=1), 0.0).astype(bf16)
            for half in halves
        ]
        places = [table[slot, p] for p in range(pages)]

        def block_of(which, j):
            return jnp.concatenate(
                [pool[which, places[j * per_block + u]] for u in range(per_block)], axis=0
            )

        scores = []
        for j in range(blocks):
            keys = block_of(0, j)
            parts = [
                lax.dot_general(
                    spread[i],
                    keys[:, i * pair_width : (i + 1) * pair_width],
                    (((1,), (1,)), ((), ())),
                    preferred_element_type=f32,
                )
                for i in range(pairs)
            ]
            score = jnp.concatenate(parts, axis=0) * scale
            scores.append(jnp.where(token_id < length - j * BLOCK, score, masked_score))
        top = scores[0]
        for score in scores[1:]:
            top = jnp.maximum(top, score)
        cache_peak = jnp.max(top, axis=1, keepdims=True)
        weights = [jnp.exp(score - cache_peak) for score in scores]
        summed = weights[0]
        for weight in weights[1:]:
            summed = summed + weight
        cache_total = jnp.sum(summed, axis=1, keepdims=True)
        full = [None] * pairs
        for j in range(blocks):
            values = block_of(1, j)
            rounded = weights[j].astype(bf16)
            for i in range(pairs):
                part = jnp.dot(
                    rounded[i * rows : (i + 1) * rows],
                    values[:, i * pair_width : (i + 1) * pair_width],
                    preferred_element_type=f32,
                )
                full[i] = part if full[i] is None else full[i] + part
        gathered = jnp.concatenate(
            [
                full[k // 2][(k % 2) * group : (k % 2 + 1) * group, (k % 2) * HD : (k % 2 + 1) * HD]
                for k in range(2 * pairs)
            ],
            axis=0,
        )
        kv_heads = 2 * pairs
        own_keys = jnp.concatenate(
            [jnp.broadcast_to(own[k : k + 1], (group, HD)) for k in range(kv_heads)], axis=0
        )
        own_values = jnp.concatenate(
            [jnp.broadcast_to(own[kv_heads + k : kv_heads + k + 1], (group, HD)) for k in range(kv_heads)],
            axis=0,
        )
        head_rows = jnp.concatenate(halves, axis=0)
        own_score = jnp.sum(head_rows * own_keys, axis=1, keepdims=True) * scale
        joint_peak = jnp.maximum(cache_peak, own_score)
        cache_weight = jnp.exp(cache_peak - joint_peak)
        own_weight = jnp.exp(own_score - joint_peak)
        numerator = cache_weight * gathered + own_weight * own_values
        attended = numerator / (cache_weight * cache_total + own_weight)
        out[...] = attended.astype(bf16)


def attend(items, plan, table, pool, extras, arrived, backs):
    heads = pool.shape[-1] // HD * (HEADS // KVH)

    def kernel(*refs):
        attend_kernel(items, arrived, *refs)

    result = pltpu.VMEM((heads, HD), bf16)
    out_shape = (pltpu.SMEM(plan.shape, jnp.int32),) + (result,) * len(items)
    if arrived:
        out_shape += (pltpu.VMEM((SLOTS, heads, HD), f32),)
    return pl.pallas_call(
        kernel,
        out_shape=out_shape,
        in_specs=[whole(pltpu.SMEM)] * 2 + [whole(pltpu.VMEM)] * (1 + len(items) + len(arrived)),
        out_specs=(whole(pltpu.SMEM),) + (whole(pltpu.VMEM),) * (len(out_shape) - 1),
        compiler_params=pltpu.CompilerParams(vmem_limit_bytes=8 * 2**20),
        cost_estimate=pl.CostEstimate(
            flops=len(items) * 4 * 1280 * 32 * 512,
            transcendentals=len(items) * 1280 * 32,
            bytes_accessed=len(items) * 2 * 80 * 16 * 1024,
        ),
    )(plan, table, *in_vmem(pool, *extras, *backs))


def rates_kernel(
    plan, conv, dt, a_log, bias, skip, x_proj, gains, rate, step_rows, drive_rows, direct
):
    gains[...] = lax.dot_general(
        x_proj[...], conv[...], (((1,), (1,)), ((), ())), preferred_element_type=f32
    )
    mixer = conv[...].astype(f32)
    step_in = dt[...].astype(f32) + bias[...]
    step = jnp.maximum(step_in, 0.0) + jnp.log1p(jnp.exp(-jnp.abs(step_in)))
    drive = step * mixer
    direct[...] = skip[...] * mixer
    for row in range(SLOTS):
        step_rows[row] = step[row : row + 1]
        drive_rows[row] = drive[row : row + 1]
    rate[...] = jnp.exp(a_log[...]) * (-LOG2E)


def rates(plan, conv, dt, a_log, bias, skip, x_proj):
    slots, width = conv.shape
    rows = pltpu.VMEM((slots, 1, width), f32)
    return pl.pallas_call(
        rates_kernel,
        out_shape=(pltpu.VMEM((x_proj.shape[0], slots), f32), pltpu.VMEM(a_log.shape, f32), rows, rows, pltpu.VMEM((slots, width), f32)),
        in_specs=[whole(pltpu.SMEM)] + [whole(pltpu.VMEM)] * 6,
        out_specs=(whole(pltpu.VMEM),) * 5,
        compiler_params=pltpu.CompilerParams(vmem_limit_bytes=8 * 2**20),
        cost_estimate=pl.CostEstimate(
            flops=10 * slots * width,
            transcendentals=a_log.size + 2 * slots * width,
            bytes_accessed=a_log.size * 4,
        ),
    )(plan, conv, dt, a_log, bias, skip, x_proj)


def update_kernel(
    plan, gains, gains_far, held, rate, step_rows, drive_rows, direct, r0, r1, r2, r3, r4,
    later, new_state, mixed,
    mixed_rows, mixed_all, out_buf, sems,
):
    moved = (r0, r1, r2, r3, r4)
    n, width = rate.shape
    for entry in range(24):
        later[entry] = plan[entry]
    coupled = gains[...] + gains_far[...]
    lane = lax.broadcasted_iota(jnp.int32, coupled.shape, 1)
    outs = []
    chunk = 1024
    for item in SEND_ORDER + (5,):
        slot = plan[8 + item]
        column = jnp.sum(jnp.where(lane == slot, coupled, 0.0), axis=1, keepdims=True)
        input_gain = jnp.broadcast_to(column[0:n], (n, 128))
        read_gain = jnp.broadcast_to(column[n : 2 * n], (n, 128))
        target = out_buf.at[item]

        def body(c, _, item=item, slot=slot, input_gain=input_gain, read_gain=read_gain, target=target):
            for u in range(chunk // 128):
                at = pl.ds(pl.multiple_of(c * chunk + u * 128, 128), 128)
                if item == 5:
                    previous = held[plan[5], :, at]
                else:
                    previous = moved[item][:, at].astype(f32)
                step_row = jnp.broadcast_to(step_rows[slot, :, at], (n, 128))
                drive_row = jnp.broadcast_to(drive_rows[slot, :, at], (n, 128))
                updated = jnp.exp2(step_row * rate[:, at]) * previous + drive_row * input_gain
                target[:, at] = updated
                mixed_rows[slot, :, at] = jnp.sum(read_gain * updated, axis=0, keepdims=True)
            return 0

        lax.fori_loop(0, width // chunk, body, 0)
        copy = pltpu.make_async_copy(target, new_state.at[slot], sems.at[item])
        copy.start()
        outs.append(copy)
    for row in range(SLOTS):
        mixed_all[row : row + 1, :] = mixed_rows[row]
    mixed[...] = (mixed_all[...] + direct[...]).astype(bf16)
    for copy in outs:
        copy.wait()


def update(plan, gains, gains_far, held, made, moved):
    slots, n, width = held.shape
    return pl.pallas_call(
        update_kernel,
        out_shape=(
            pltpu.SMEM(plan.shape, jnp.int32),
            pltpu.HBM(held.shape, f32),
            pltpu.VMEM((slots, width), bf16),
        ),
        in_specs=[whole(pltpu.SMEM)] + [whole(pltpu.VMEM)] * (7 + BITS),
        out_specs=(whole(pltpu.SMEM), whole(pl.ANY), whole(pltpu.VMEM)),
        scratch_shapes=[
            pltpu.VMEM((slots, 1, width), f32),
            pltpu.VMEM((slots, width), f32),
            pltpu.VMEM((slots, n, width), f32),
            pltpu.SemaphoreType.DMA((slots,)),
        ],
        compiler_params=pltpu.CompilerParams(vmem_limit_bytes=8 * 2**20),
        cost_estimate=pl.CostEstimate(
            flops=held.size * 8, transcendentals=held.size, bytes_accessed=held.size * 6
        ),
    )(plan, *in_vmem(gains, gains_far, held, *made, *moved))


def place_kernel(plan, placed, *refs):
    backs, (mixed, attended, handed, head_rows, rows, rounded, sems) = refs[: len(LAST)], refs[len(LAST) :]
    through = pltpu.make_async_copy(mixed, handed, sems.at[0])
    through.start()
    head_rows[...] = placed[...]
    for item, back in zip(LAST, backs):
        head_rows[plan[8 + item]] = back[...].astype(f32)
    for slot in range(SLOTS):
        for h in range(head_rows.shape[1]):
            rows[slot : slot + 1, h * HD : (h + 1) * HD] = head_rows[slot, h : h + 1, :]
    rounded[...] = rows[...].astype(bf16)
    out = pltpu.make_async_copy(rounded, attended, sems.at[1])
    out.start()
    through.wait()
    out.wait()


def place(plan, placed, backs, mixed):
    heads = placed.shape[1]
    shape = (SLOTS, heads * HD)
    return pl.pallas_call(
        place_kernel,
        out_shape=(pltpu.HBM(shape, bf16), pltpu.HBM(mixed.shape, bf16)),
        in_specs=[whole(pltpu.SMEM)] + [whole(pltpu.VMEM)] * (len(backs) + 2),
        out_specs=(whole(pl.ANY),) * 2,
        scratch_shapes=[
            pltpu.VMEM(placed.shape, f32),
            pltpu.VMEM(shape, f32),
            pltpu.VMEM(shape, bf16),
            pltpu.SemaphoreType.DMA((2,)),
        ],
    )(plan, *in_vmem(placed, *backs, mixed))


def per_device(
    source_slot,
    lengths,
    block_table,
    queries,
    kv_pool,
    new_kv,
    ssm_state,
    conv_out,
    dt_raw,
    x_proj,
    a_log,
    dt_bias,
    skip_gain,
):
    fresh = jnp.transpose(new_kv[0], (1, 0, 2))
    plan, held, heads = load(source_slot, lengths, ssm_state[0], queries[0], fresh)
    packs = pack(plan, held, heads)
    moved = [None] * BITS
    for bit in SEND_ORDER:
        moved[bit] = swapped(packs[bit], "replica", bit)
    gains, *made = rates(
        plan, conv_out[0], dt_raw[0], a_log[0], dt_bias, skip_gain, x_proj[0]
    )
    gains_far = swapped(gains, "tensor", 0)
    extras = moved + [heads]
    pool = kv_pool[0]
    plan, *attended = attend(FIRST, plan, block_table, pool, [extras[i] for i in FIRST], (), ())
    backs = [across(value, item) for item, value in zip(FIRST, attended)]
    plan, new_state, mixed = update(plan, gains, gains_far, held, made, moved)
    handed_mamba = across(mixed, BITS)
    plan, *attended, placed = attend(
        LAST, plan, block_table, pool, [extras[i] for i in LAST], FIRST, backs
    )
    backs = [across(value, item) for item, value in zip(LAST, attended)]
    handed_attention, handed_mamba = place(plan, placed, backs, handed_mamba)
    return handed_mamba[None], handed_attention[None], new_state[None]


def solution(mesh):
    in_specs = (
        P(),
        P(),
        P("replica", None),
        P("section", "replica", "tensor"),
        P("section", None, "replica", None, "tensor"),
        P("section", None, "replica", "tensor"),
        P("section", "replica", None, "tensor"),
        P("section", "replica", "tensor"),
        P("section", "replica", "tensor"),
        P("section", None, "tensor"),
        P("section", None, "tensor"),
        P("section", "tensor"),
        P("section", "tensor"),
    )
    out_specs = (
        P("section", "replica", "tensor"),
        P("section", "replica", "tensor"),
        P("section", "replica", None, "tensor"),
    )
    return jax.shard_map(
        per_device, mesh=mesh, in_specs=in_specs, out_specs=out_specs, check_vma=False
    )
```

```python
import jax
import jax.numpy as jnp
from jax import lax
from jax.experimental import pallas as pl
from jax.experimental.pallas import tpu as pltpu
from jax.sharding import PartitionSpec as P

HEADS = 64
KVH = 8
HD = 128

SLOTS = 6
BITS = 5
FAR = (2, 4)
NEAR = (1, 3, 0)
FIRST = (BITS,) + FAR
BLOCK = 256
LOG2E = 1.4426950408889634
WEIGHT = 10**10

masked_score = -1e30
f32 = jnp.float32
bf16 = jnp.bfloat16


def swapped(value, axis, bit):
    mask = 2**bit
    pairs = [(source, source ^ mask) for source in range(lax.axis_size(axis))]
    return lax.ppermute(value, axis, pairs)


def across(value, bit):
    sections, replicas = lax.axis_size("section"), lax.axis_size("replica")
    mask = 2**bit if bit < BITS else 0
    pairs = [
        (s * replicas + r, ((s + 1) % sections) * replicas + (r ^ mask))
        for s in range(sections)
        for r in range(replicas)
    ]
    return lax.ppermute(value, ("section", "replica"), pairs)


def whole(space):
    return pl.BlockSpec(memory_space=space)


def in_hbm(*values):
    return [pltpu.with_memory_space_constraint(value, pltpu.HBM) for value in values]


def in_vmem(*values):
    return [pltpu.with_memory_space_constraint(value, pltpu.VMEM) for value in values]


def write_plan(own, src, lens, plan):
    first = own * SLOTS
    for entry in range(24):
        plan[entry] = 0
    for bit in range(BITS):
        partner = jnp.bitwise_xor(own, 1 << bit) * SLOTS
        leave = jnp.int32(0)
        served = jnp.int32(1)
        ask = jnp.int32(0)
        for j in range(SLOTS):
            there = src[partner + j] - first
            gives = (there >= 0) & (there < SLOTS)
            leave = jnp.where(gives, there, leave)
            served = jnp.where(gives, lens[partner + j], served)
            here = src[first + j] - partner
            ask = jnp.where((here >= 0) & (here < SLOTS), j, ask)
        plan[bit] = leave
        plan[8 + bit] = ask
        plan[16 + bit] = served
    kept_old = jnp.int32(0)
    kept_new = jnp.int32(0)
    for j in range(SLOTS):
        here = src[first + j] - first
        stays = (here >= 0) & (here < SLOTS)
        kept_old = jnp.where(stays, here, kept_old)
        kept_new = jnp.where(stays, j, kept_new)
    plan[5] = kept_old
    plan[13] = kept_new
    plan[21] = lens[first + kept_new]


def load_kernel(
    src_in, lens_in, table_in, queries, fresh, conv, x_proj, plan, table, gains, heads_out, far0, far1,
    src, lens, q_buf, fresh_buf, conv_buf, x_buf, head_rows, own_rows, sems,
):
    copies = [
        pltpu.make_async_copy(source, target, sems.at[i])
        for i, (source, target) in enumerate(
            (
                (src_in, src), (lens_in, lens), (queries, q_buf), (fresh, fresh_buf),
                (table_in, table), (conv, conv_buf), (x_proj, x_buf),
            )
        )
    ]
    for copy in copies:
        copy.start()
    copies[0].wait()
    copies[1].wait()
    write_plan(lax.axis_index("replica"), src, lens, plan)
    copies[2].wait()
    copies[3].wait()
    heads = head_rows.shape[1]
    half = heads // 2
    keys = fresh_buf.shape[-1] // HD
    own_rows[...] = jnp.zeros_like(own_rows)
    for h in range(heads):
        column = q_buf[:, h * HD : (h + 1) * HD].astype(f32)
        for slot in range(SLOTS):
            head_rows[slot, h : h + 1, :] = column[slot : slot + 1]
    for item in range(BITS + 1):
        slot = plan[8 + item]
        pair = fresh_buf[slot].astype(f32)
        for k in range(keys):
            own_rows[k : k + 1, :] = pair[0:1, k * HD : (k + 1) * HD]
            own_rows[keys + k : keys + k + 1, :] = pair[1:2, k * HD : (k + 1) * HD]
        heads_out[item] = jnp.concatenate(
            [head_rows[slot, 0:half], head_rows[slot, half:heads], own_rows[...]], axis=1
        ).astype(bf16)
    for bit, out in zip(FAR, (far0, far1)):
        out[...] = heads_out[bit]
    copies[4].wait()
    copies[5].wait()
    copies[6].wait()
    gains[...] = lax.dot_general(
        x_buf[...], conv_buf[...], (((1,), (1,)), ((), ())), preferred_element_type=f32
    )


def load(source_slot, lengths, block_table, queries, fresh, conv, x_proj):
    heads = queries.shape[1] // HD
    half = heads // 2
    return pl.pallas_call(
        load_kernel,
        out_shape=(
            pltpu.SMEM((24,), jnp.int32),
            pltpu.SMEM(block_table.shape, jnp.int32),
            pltpu.VMEM((x_proj.shape[0], SLOTS), f32),
            pltpu.VMEM((BITS + 1, half, 3 * HD), bf16),
        )
        + (pltpu.VMEM((half, 3 * HD), bf16),) * len(FAR),
        in_specs=[whole(pl.ANY)] * 7,
        out_specs=(whole(pltpu.SMEM),) * 2 + (whole(pltpu.VMEM),) * (2 + len(FAR)),
        scratch_shapes=[
            pltpu.SMEM(source_slot.shape, jnp.int32),
            pltpu.SMEM(lengths.shape, jnp.int32),
            pltpu.VMEM(queries.shape, bf16),
            pltpu.VMEM(fresh.shape, bf16),
            pltpu.VMEM(conv.shape, bf16),
            pltpu.VMEM(x_proj.shape, bf16),
            pltpu.VMEM((SLOTS, heads, HD), f32),
            pltpu.VMEM((half, HD), f32),
            pltpu.SemaphoreType.DMA((7,)),
        ],
        compiler_params=pltpu.CompilerParams(vmem_limit_bytes=4 * 2**20),
        cost_estimate=pl.CostEstimate(flops=WEIGHT, transcendentals=0, bytes_accessed=queries.size * 2),
    )(*in_hbm(source_slot, lengths, block_table, queries, fresh, conv, x_proj))


def pack_kernel(plan, held, heads, later, *packs):
    width = held.shape[-1]
    for entry in range(24):
        later[entry] = plan[entry]
    for bit, out in zip(NEAR, packs):
        out[:, :width] = held[plan[bit]].astype(bf16)
        out[:, width:] = heads[bit]


def pack(plan, held, heads):
    n, width = held.shape[1:]
    return pl.pallas_call(
        pack_kernel,
        out_shape=(pltpu.SMEM(plan.shape, jnp.int32),)
        + (pltpu.VMEM((n, width + heads.shape[-1]), bf16),) * len(NEAR),
        in_specs=[whole(pltpu.SMEM)] + [whole(pltpu.VMEM)] * 2,
        out_specs=(whole(pltpu.SMEM),) + (whole(pltpu.VMEM),) * len(NEAR),
        compiler_params=pltpu.CompilerParams(vmem_limit_bytes=4 * 2**20),
        cost_estimate=pl.CostEstimate(
            flops=0, transcendentals=0, bytes_accessed=held.size * 3
        ),
    )(plan, *in_vmem(held, heads))


def attend_items(items, plan, table, pool, extras, outs):
    page = pool.shape[2]
    pages = table.shape[1]
    per_block = BLOCK // page
    blocks = pages // per_block
    pair_width = 2 * HD
    pairs = pool.shape[3] // pair_width
    group = HEADS // KVH
    rows = 2 * group
    kv_heads = 2 * pairs
    scale = HD ** (-0.5)
    row_id = lax.broadcasted_iota(jnp.int32, (rows, pair_width), 0)
    lane_id = lax.broadcasted_iota(jnp.int32, (rows, pair_width), 1)
    own_block = (row_id < group) == (lane_id < HD)
    token_id = lax.broadcasted_iota(jnp.int32, (rows * pairs, BLOCK), 1)

    def block_of(which, places, j):
        return jnp.concatenate(
            [pool[which, places[j * per_block + u]] for u in range(per_block)], axis=0
        )

    def places_of(item):
        slot = plan[item]
        return [table[slot, p] for p in range(pages)]

    def halves_of(extra):
        base = extra.shape[1] - 3 * HD
        return [extra[:, base + i * HD : base + (i + 1) * HD] for i in range(2)]

    def score_block(spread, length, places, j):
        keys = block_of(0, places, j)
        parts = [
            lax.dot_general(
                spread[i],
                keys[:, i * pair_width : (i + 1) * pair_width],
                (((1,), (1,)), ((), ())),
                preferred_element_type=f32,
            )
            for i in range(pairs)
        ]
        score = jnp.concatenate(parts, axis=0) * scale
        return jnp.where(token_id < length - j * BLOCK, score, masked_score)

    def ready(item, extra):
        spread = [
            jnp.where(own_block, jnp.concatenate([half, half], axis=1).astype(f32), 0.0).astype(bf16)
            for half in halves_of(extra)
        ]
        return spread, plan[16 + item], places_of(item)

    current = ready(items[0], extras[0])
    scores = [score_block(*current, j) for j in range(blocks)]
    for at, (extra, out) in enumerate(zip(extras, outs)):
        places = current[2]
        top = scores[0]
        for score in scores[1:]:
            top = jnp.maximum(top, score)
        cache_peak = jnp.max(top, axis=1, keepdims=True)
        weights = [jnp.exp(score - cache_peak) for score in scores]
        summed = weights[0]
        for weight in weights[1:]:
            summed = summed + weight
        cache_total = jnp.sum(summed, axis=1, keepdims=True)
        following = at + 1 < len(items)
        if following:
            current = ready(items[at + 1], extras[at + 1])
        scores = []
        full = [None] * pairs
        for j in range(blocks):
            if following:
                scores.append(score_block(*current, j))
            values = block_of(1, places, j)
            rounded = weights[j].astype(bf16)
            for i in range(pairs):
                part = jnp.dot(
                    rounded[i * rows : (i + 1) * rows],
                    values[:, i * pair_width : (i + 1) * pair_width],
                    preferred_element_type=f32,
                )
                full[i] = part if full[i] is None else full[i] + part
        gathered = jnp.concatenate(
            [
                full[k // 2][(k % 2) * group : (k % 2 + 1) * group, (k % 2) * HD : (k % 2 + 1) * HD]
                for k in range(kv_heads)
            ],
            axis=0,
        )
        own = extra[:, extra.shape[1] - HD :].astype(f32)
        own_keys = jnp.concatenate(
            [jnp.broadcast_to(own[k : k + 1], (group, HD)) for k in range(kv_heads)], axis=0
        )
        own_values = jnp.concatenate(
            [jnp.broadcast_to(own[kv_heads + k : kv_heads + k + 1], (group, HD)) for k in range(kv_heads)],
            axis=0,
        )
        head_rows = jnp.concatenate(halves_of(extra), axis=0).astype(f32)
        own_score = jnp.sum(head_rows * own_keys, axis=1, keepdims=True) * scale
        joint_peak = jnp.maximum(cache_peak, own_score)
        cache_weight = jnp.exp(cache_peak - joint_peak)
        own_weight = jnp.exp(own_score - joint_peak)
        numerator = cache_weight * gathered + own_weight * own_values
        attended = numerator / (cache_weight * cache_total + own_weight)
        out(attended)


def rates_kernel(plan, conv, dt, a_log, bias, skip, rate, step_rows, drive_rows, direct):
    mixer = conv[...].astype(f32)
    step_in = dt[...].astype(f32) + bias[...]
    step = jnp.maximum(step_in, 0.0) + jnp.log1p(jnp.exp(-jnp.abs(step_in)))
    drive = step * mixer
    direct[...] = skip[...] * mixer
    for row in range(SLOTS):
        step_rows[row] = step[row : row + 1]
        drive_rows[row] = drive[row : row + 1]
    rate[...] = jnp.exp(a_log[...]) * (-LOG2E)


def rates(plan, conv, dt, a_log, bias, skip):
    slots, width = conv.shape
    rows = pltpu.VMEM((slots, 1, width), f32)
    return pl.pallas_call(
        rates_kernel,
        out_shape=(pltpu.VMEM(a_log.shape, f32), rows, rows, pltpu.VMEM((slots, width), f32)),
        in_specs=[whole(pltpu.SMEM)] + [whole(pltpu.VMEM)] * 5,
        out_specs=(whole(pltpu.VMEM),) * 4,
        compiler_params=pltpu.CompilerParams(vmem_limit_bytes=8 * 2**20),
        cost_estimate=pl.CostEstimate(
            flops=10 * slots * width,
            transcendentals=a_log.size + 2 * slots * width,
            bytes_accessed=a_log.size * 4,
        ),
    )(plan, conv, dt, a_log, bias, skip)


def update_items(
    items, plan, gains, rate, step_rows, drive_rows, held, moved, new_state, mixed_rows, out_buf, sems
):
    n, width = rate.shape
    coupled = gains[...]
    lane = lax.broadcasted_iota(jnp.int32, coupled.shape, 1)
    copies = []
    for i, item in enumerate(items):
        slot = plan[8 + item]
        column = jnp.sum(jnp.where(lane == slot, coupled, 0.0), axis=1, keepdims=True)
        input_gain = jnp.broadcast_to(column[0:n], (n, HD))
        read_gain = jnp.broadcast_to(column[n : 2 * n], (n, HD))
        for c in range(0, width, HD):
            at = slice(c, c + HD)
            previous = held[plan[BITS], :, at] if item == BITS else moved[i][:, at].astype(f32)
            step_row = jnp.broadcast_to(step_rows[slot, :, at], (n, HD))
            drive_row = jnp.broadcast_to(drive_rows[slot, :, at], (n, HD))
            updated = jnp.exp2(step_row * rate[:, at]) * previous + drive_row * input_gain
            out_buf[i, :, at] = updated
            mixed_rows[slot, :, at] = jnp.sum(read_gain * updated, axis=0, keepdims=True)
        copies.append(pltpu.make_async_copy(out_buf.at[i], new_state.at[slot], sems.at[i]))
        copies[-1].start()
    return copies


def first_kernel(
    plan, table, pool, held, heads, q0, q1, gains, gains_far, later, coupled, own, row0, row1
):
    width = held.shape[-1]
    coupled[...] = gains[...] + gains_far[...]
    for entry in range(24):
        later[entry] = plan[entry]

    def keep(attended):
        own[...] = attended.astype(bf16)

    def into(row):
        def put(attended):
            half = attended.shape[0] // 2
            row[:, width : width + HD] = attended[:half].astype(bf16)
            row[:, width + HD :] = attended[half:].astype(bf16)

        return put

    attend_items(FIRST, plan, table, pool, [heads.at[BITS], q0, q1], [keep, into(row0), into(row1)])
    for bit, row in zip(FAR, (row0, row1)):
        row[:, :width] = held[plan[bit]].astype(bf16)


def attention_cost(count):
    return dict(
        flops=count * 4 * 1280 * 32 * 512,
        transcendentals=count * 1280 * 32,
        bytes_accessed=count * 2 * 80 * 16 * 1024,
    )


def first(plan, table, pool, held, heads, gains, gains_far, queries):
    n, width = held.shape[1:]
    result = pltpu.VMEM((2 * n, HD), bf16)
    return pl.pallas_call(
        first_kernel,
        out_shape=(pltpu.SMEM(plan.shape, jnp.int32), pltpu.VMEM(gains.shape, f32), result)
        + (pltpu.VMEM((n, width + 2 * HD), bf16),) * len(FAR),
        in_specs=[whole(pltpu.SMEM)] * 2 + [whole(pltpu.VMEM)] * (5 + len(FAR)),
        out_specs=(whole(pltpu.SMEM),) + (whole(pltpu.VMEM),) * (2 + len(FAR)),
        compiler_params=pltpu.CompilerParams(vmem_limit_bytes=8 * 2**20),
        cost_estimate=pl.CostEstimate(**attention_cost(len(FIRST))),
    )(plan, table, *in_vmem(pool, held, heads, *queries, gains, gains_far))


def near_kernel(
    plan, table, pool, gains, rate, step_rows, drive_rows, held, x0, x1, x2,
    later, new_state, mixed_rows, a0, a1, a2,
    out_buf, sems,
):
    for entry in range(24):
        later[entry] = plan[entry]
    extras = [x0, x1, x2]
    copies = update_items(
        (BITS,) + NEAR, plan, gains, rate, step_rows, drive_rows, held, [None] + extras,
        new_state, mixed_rows, out_buf, sems,
    )

    def into(out):
        def put(attended):
            out[...] = attended.astype(bf16)

        return put

    attend_items(NEAR, plan, table, pool, extras, [into(a0), into(a1), into(a2)])
    for copy in copies:
        copy.wait()


def near(plan, table, pool, gains, made, held, extras):
    slots, n, width = held.shape
    count = 1 + len(NEAR)
    inputs = in_vmem(pool, gains, *made[:3], held, *extras)
    return pl.pallas_call(
        near_kernel,
        out_shape=(
            pltpu.SMEM(plan.shape, jnp.int32),
            pltpu.HBM(held.shape, f32),
            pltpu.VMEM((slots, 1, width), f32),
        )
        + (pltpu.VMEM((2 * n, HD), bf16),) * len(NEAR),
        in_specs=[whole(pltpu.SMEM)] * 2 + [whole(pltpu.VMEM)] * len(inputs),
        out_specs=(whole(pltpu.SMEM), whole(pl.ANY)) + (whole(pltpu.VMEM),) * (1 + len(NEAR)),
        scratch_shapes=[pltpu.VMEM((count, n, width), f32), pltpu.SemaphoreType.DMA((count,))],
        compiler_params=pltpu.CompilerParams(vmem_limit_bytes=8 * 2**20),
        cost_estimate=pl.CostEstimate(**attention_cost(len(NEAR))),
    )(plan, table, *inputs)


def last_kernel(
    plan, gains, rate, step_rows, drive_rows, direct, own, x0, x1, b0, b1, b2, state_before, rows_before,
    later, new_state, mixed_rows, final, placed,
    mixed_all, out_buf, sems,
):
    for entry in range(24):
        later[entry] = plan[entry]
    slots, width = direct.shape
    copies = update_items(
        FAR, plan, gains, rate, step_rows, drive_rows, None, [x0, x1],
        new_state, mixed_rows, out_buf, sems,
    )
    mixed_all[...] = jnp.zeros_like(mixed_all)
    for slot in range(slots):
        mixed_all[slot : slot + 1, :] = mixed_rows[slot] + direct[slot : slot + 1, :]
    final[:, :width] = mixed_all[...].astype(bf16)
    results = [own[...].astype(f32)]
    for row in (x0, x1):
        results.append(
            jnp.concatenate([row[:, width : width + HD], row[:, width + HD :]], axis=0).astype(f32)
        )
    for i, result in enumerate(results):
        for k in range(result.shape[0] // 8):
            start = width + (4 * i + k) * HD
            final[:, start : start + HD] = result[8 * k : 8 * k + 8].astype(bf16)
    for item, back in zip(NEAR, (b0, b1, b2)):
        placed[plan[8 + item]] = back[...].astype(f32)
    for copy in copies:
        copy.wait()


def last(plan, gains, made, own, extras, backs, new_state, mixed_rows):
    slots, width = made[3].shape
    n = made[0].shape[0]
    inputs = in_vmem(gains, *made, own, *extras, *backs) + in_hbm(new_state) + in_vmem(mixed_rows)
    vmem = whole(pltpu.VMEM)
    return pl.pallas_call(
        last_kernel,
        out_shape=(
            pltpu.SMEM(plan.shape, jnp.int32),
            pltpu.HBM(new_state.shape, f32),
            pltpu.VMEM(mixed_rows.shape, f32),
            pltpu.VMEM((8, width + 12 * HD), bf16),
            pltpu.VMEM((slots, 2 * n, HD), f32),
        ),
        in_specs=[whole(pltpu.SMEM)] + [vmem] * (len(inputs) - 2) + [whole(pl.ANY), vmem],
        out_specs=(whole(pltpu.SMEM), whole(pl.ANY), vmem, vmem, vmem),
        scratch_shapes=[
            pltpu.VMEM((8, width), f32),
            pltpu.VMEM((len(FAR), n, width), f32),
            pltpu.SemaphoreType.DMA((len(FAR),)),
        ],
        input_output_aliases={len(inputs) - 1: 1, len(inputs): 2},
        compiler_params=pltpu.CompilerParams(vmem_limit_bytes=8 * 2**20),
        cost_estimate=pl.CostEstimate(
            flops=16 * n * width, transcendentals=2 * n * width, bytes_accessed=12 * n * width
        ),
    )(plan, *inputs)


def place_kernel(plan, final, placed, attended, handed, head_rows, rows, rounded, mixed, sems):
    slots, width = mixed.shape
    mixed[...] = final[:, :width][0:slots]
    through = pltpu.make_async_copy(mixed, handed, sems.at[0])
    through.start()
    head_rows[...] = placed[...]
    for i, item in enumerate(FIRST):
        for k in range(head_rows.shape[1] // 8):
            start = width + (4 * i + k) * HD
            head_rows[plan[8 + item], 8 * k : 8 * k + 8] = final[:, start : start + HD].astype(f32)
    for slot in range(slots):
        for h in range(head_rows.shape[1]):
            rows[slot : slot + 1, h * HD : (h + 1) * HD] = head_rows[slot, h : h + 1, :]
    rounded[...] = rows[...].astype(bf16)
    out = pltpu.make_async_copy(rounded, attended, sems.at[1])
    out.start()
    through.wait()
    out.wait()


def place(plan, final, placed):
    heads = placed.shape[1]
    shape = (SLOTS, heads * HD)
    mixed = (SLOTS, final.shape[1] - 12 * HD)
    return pl.pallas_call(
        place_kernel,
        out_shape=(pltpu.HBM(shape, bf16), pltpu.HBM(mixed, bf16)),
        in_specs=[whole(pltpu.SMEM)] + [whole(pltpu.VMEM)] * 2,
        out_specs=(whole(pl.ANY),) * 2,
        scratch_shapes=[
            pltpu.VMEM((SLOTS, heads, HD), f32),
            pltpu.VMEM(shape, f32),
            pltpu.VMEM(shape, bf16),
            pltpu.VMEM(mixed, bf16),
            pltpu.SemaphoreType.DMA((2,)),
        ],
    )(plan, *in_vmem(final, placed))


def per_device(
    source_slot,
    lengths,
    block_table,
    queries,
    kv_pool,
    new_kv,
    ssm_state,
    conv_out,
    dt_raw,
    x_proj,
    a_log,
    dt_bias,
    skip_gain,
):
    fresh = jnp.transpose(new_kv[0], (1, 0, 2))
    held = ssm_state[0]
    pool = kv_pool[0]
    plan, table, gains, heads, *queries_far = load(
        source_slot, lengths, block_table, queries[0], fresh, conv_out[0], x_proj[0]
    )
    gains_far = swapped(gains, "tensor", 0)
    queries_far = [swapped(value, "replica", bit) for bit, value in zip(FAR, queries_far)]
    plan, *rows = pack(plan, held, heads)
    rows_near = [swapped(value, "replica", bit) for bit, value in zip(NEAR, rows)]
    plan, gains, own, *rows = first(plan, table, pool, held, heads, gains, gains_far, queries_far)
    rows_far = [swapped(value, "replica", bit) for bit, value in zip(FAR, rows)]
    made = rates(plan, conv_out[0], dt_raw[0], a_log[0], dt_bias, skip_gain)
    plan, new_state, mixed_rows, *attended = near(plan, table, pool, gains, made, held, rows_near)
    backs = [across(value, bit) for bit, value in zip(NEAR, attended)]
    plan, new_state, _, final, placed = last(
        plan, gains, made, own, rows_far, backs, new_state, mixed_rows
    )
    handed_attention, handed_mamba = place(plan, across(final, BITS), placed)
    return handed_mamba[None], handed_attention[None], new_state[None]


def solution(mesh):
    in_specs = (
        P(),
        P(),
        P("replica", None),
        P("section", "replica", "tensor"),
        P("section", None, "replica", None, "tensor"),
        P("section", None, "replica", "tensor"),
        P("section", "replica", None, "tensor"),
        P("section", "replica", "tensor"),
        P("section", "replica", "tensor"),
        P("section", None, "tensor"),
        P("section", None, "tensor"),
        P("section", "tensor"),
        P("section", "tensor"),
    )
    out_specs = (
        P("section", "replica", "tensor"),
        P("section", "replica", "tensor"),
        P("section", "replica", None, "tensor"),
    )
    return jax.shard_map(
        per_device, mesh=mesh, in_specs=in_specs, out_specs=out_specs, check_vma=False
    )
```

```python
import jax
import jax.numpy as jnp
from jax import lax
from jax.experimental import pallas as pl
from jax.experimental.pallas import tpu as pltpu
from jax.sharding import PartitionSpec as P

HEADS = 64
KVH = 8
HD = 128

SLOTS = 6
BITS = 5
FAR = (2, 4)
NEAR = (1, 3, 0)
FIRST = (BITS,) + FAR
BLOCK = 256
LOG2E = 1.4426950408889634
WEIGHT = 10**10

masked_score = -1e30
f32 = jnp.float32
bf16 = jnp.bfloat16


def swapped(value, axis, bit):
    mask = 2**bit
    pairs = [(source, source ^ mask) for source in range(lax.axis_size(axis))]
    return lax.ppermute(value, axis, pairs)


def across(value, bit):
    sections, replicas = lax.axis_size("section"), lax.axis_size("replica")
    mask = 2**bit if bit < BITS else 0
    pairs = [
        (s * replicas + r, ((s + 1) % sections) * replicas + (r ^ mask))
        for s in range(sections)
        for r in range(replicas)
    ]
    return lax.ppermute(value, ("section", "replica"), pairs)


def whole(space):
    return pl.BlockSpec(memory_space=space)


def in_hbm(*values):
    return [pltpu.with_memory_space_constraint(value, pltpu.HBM) for value in values]


def in_vmem(*values):
    return [pltpu.with_memory_space_constraint(value, pltpu.VMEM) for value in values]


def write_plan(own, src, lens, plan):
    first = own * SLOTS
    for entry in range(24):
        plan[entry] = 0
    for bit in range(BITS):
        partner = jnp.bitwise_xor(own, 1 << bit) * SLOTS
        leave = jnp.int32(0)
        served = jnp.int32(1)
        ask = jnp.int32(0)
        for j in range(SLOTS):
            there = src[partner + j] - first
            gives = (there >= 0) & (there < SLOTS)
            leave = jnp.where(gives, there, leave)
            served = jnp.where(gives, lens[partner + j], served)
            here = src[first + j] - partner
            ask = jnp.where((here >= 0) & (here < SLOTS), j, ask)
        plan[bit] = leave
        plan[8 + bit] = ask
        plan[16 + bit] = served
    kept_old = jnp.int32(0)
    kept_new = jnp.int32(0)
    for j in range(SLOTS):
        here = src[first + j] - first
        stays = (here >= 0) & (here < SLOTS)
        kept_old = jnp.where(stays, here, kept_old)
        kept_new = jnp.where(stays, j, kept_new)
    plan[5] = kept_old
    plan[13] = kept_new
    plan[21] = lens[first + kept_new]


def load_kernel(
    src_in, lens_in, table_in, queries, fresh, conv, x_proj, plan, table, gains, heads_out, far0, far1,
    src, lens, q_buf, fresh_buf, conv_buf, x_buf, head_rows, own_rows, sems,
):
    copies = [
        pltpu.make_async_copy(source, target, sems.at[i])
        for i, (source, target) in enumerate(
            (
                (src_in, src), (lens_in, lens), (queries, q_buf), (fresh, fresh_buf),
                (table_in, table), (conv, conv_buf), (x_proj, x_buf),
            )
        )
    ]
    for copy in copies:
        copy.start()
    copies[0].wait()
    copies[1].wait()
    write_plan(lax.axis_index("replica"), src, lens, plan)
    copies[2].wait()
    copies[3].wait()
    heads = head_rows.shape[1]
    half = heads // 2
    keys = fresh_buf.shape[-1] // HD
    own_rows[...] = jnp.zeros_like(own_rows)
    for h in range(heads):
        column = q_buf[:, h * HD : (h + 1) * HD].astype(f32)
        for slot in range(SLOTS):
            head_rows[slot, h : h + 1, :] = column[slot : slot + 1]
    for item in range(BITS + 1):
        slot = plan[8 + item]
        pair = fresh_buf[slot].astype(f32)
        for k in range(keys):
            own_rows[k : k + 1, :] = pair[0:1, k * HD : (k + 1) * HD]
            own_rows[keys + k : keys + k + 1, :] = pair[1:2, k * HD : (k + 1) * HD]
        heads_out[item] = jnp.concatenate(
            [head_rows[slot, 0:half], head_rows[slot, half:heads], own_rows[...]], axis=1
        ).astype(bf16)
    for bit, out in zip(FAR, (far0, far1)):
        out[...] = heads_out[bit]
    copies[4].wait()
    copies[5].wait()
    copies[6].wait()
    gains[...] = lax.dot_general(
        x_buf[...], conv_buf[...], (((1,), (1,)), ((), ())), preferred_element_type=f32
    )


def load(source_slot, lengths, block_table, queries, fresh, conv, x_proj):
    heads = queries.shape[1] // HD
    half = heads // 2
    return pl.pallas_call(
        load_kernel,
        out_shape=(
            pltpu.SMEM((24,), jnp.int32),
            pltpu.SMEM(block_table.shape, jnp.int32),
            pltpu.VMEM((x_proj.shape[0], SLOTS), f32),
            pltpu.VMEM((BITS + 1, half, 3 * HD), bf16),
        )
        + (pltpu.VMEM((half, 3 * HD), bf16),) * len(FAR),
        in_specs=[whole(pl.ANY)] * 7,
        out_specs=(whole(pltpu.SMEM),) * 2 + (whole(pltpu.VMEM),) * (2 + len(FAR)),
        scratch_shapes=[
            pltpu.SMEM(source_slot.shape, jnp.int32),
            pltpu.SMEM(lengths.shape, jnp.int32),
            pltpu.VMEM(queries.shape, bf16),
            pltpu.VMEM(fresh.shape, bf16),
            pltpu.VMEM(conv.shape, bf16),
            pltpu.VMEM(x_proj.shape, bf16),
            pltpu.VMEM((SLOTS, heads, HD), f32),
            pltpu.VMEM((half, HD), f32),
            pltpu.SemaphoreType.DMA((7,)),
        ],
        compiler_params=pltpu.CompilerParams(vmem_limit_bytes=4 * 2**20),
        cost_estimate=pl.CostEstimate(flops=WEIGHT, transcendentals=0, bytes_accessed=queries.size * 2),
    )(*in_hbm(source_slot, lengths, block_table, queries, fresh, conv, x_proj))


def pack_kernel(plan, held, heads, later, *packs):
    width = held.shape[-1]
    for entry in range(24):
        later[entry] = plan[entry]
    for bit, out in zip(NEAR, packs):
        out[:, :width] = held[plan[bit]].astype(bf16)
        out[:, width:] = heads[bit]


def pack(plan, held, heads):
    n, width = held.shape[1:]
    return pl.pallas_call(
        pack_kernel,
        out_shape=(pltpu.SMEM(plan.shape, jnp.int32),)
        + (pltpu.VMEM((n, width + heads.shape[-1]), bf16),) * len(NEAR),
        in_specs=[whole(pltpu.SMEM)] + [whole(pltpu.VMEM)] * 2,
        out_specs=(whole(pltpu.SMEM),) + (whole(pltpu.VMEM),) * len(NEAR),
        compiler_params=pltpu.CompilerParams(vmem_limit_bytes=4 * 2**20),
        cost_estimate=pl.CostEstimate(
            flops=0, transcendentals=0, bytes_accessed=held.size * 3
        ),
    )(plan, *in_vmem(held, heads))


def attend_items(items, plan, table, pool, extras, outs):
    page = pool.shape[2]
    pages = table.shape[1]
    per_block = BLOCK // page
    blocks = pages // per_block
    pair_width = 2 * HD
    pairs = pool.shape[3] // pair_width
    group = HEADS // KVH
    rows = 2 * group
    kv_heads = 2 * pairs
    scale = HD ** (-0.5)
    row_id = lax.broadcasted_iota(jnp.int32, (rows, pair_width), 0)
    lane_id = lax.broadcasted_iota(jnp.int32, (rows, pair_width), 1)
    own_block = (row_id < group) == (lane_id < HD)
    token_id = lax.broadcasted_iota(jnp.int32, (rows * pairs, BLOCK), 1)

    def block_of(which, places, j):
        return jnp.concatenate(
            [pool[which, places[j * per_block + u]] for u in range(per_block)], axis=0
        )

    def places_of(item):
        slot = plan[item]
        return [table[slot, p] for p in range(pages)]

    def halves_of(extra):
        base = extra.shape[1] - 3 * HD
        return [extra[:, base + i * HD : base + (i + 1) * HD] for i in range(2)]

    def score_block(spread, length, places, j):
        keys = block_of(0, places, j)
        parts = [
            lax.dot_general(
                spread[i],
                keys[:, i * pair_width : (i + 1) * pair_width],
                (((1,), (1,)), ((), ())),
                preferred_element_type=f32,
            )
            for i in range(pairs)
        ]
        score = jnp.concatenate(parts, axis=0) * scale
        return jnp.where(token_id < length - j * BLOCK, score, masked_score)

    def ready(item, extra):
        spread = [
            jnp.where(own_block, jnp.concatenate([half, half], axis=1).astype(f32), 0.0).astype(bf16)
            for half in halves_of(extra)
        ]
        return spread, plan[16 + item], places_of(item)

    current = ready(items[0], extras[0])
    scores = [score_block(*current, j) for j in range(blocks)]
    for at, (extra, out) in enumerate(zip(extras, outs)):
        places = current[2]
        top = scores[0]
        for score in scores[1:]:
            top = jnp.maximum(top, score)
        cache_peak = jnp.max(top, axis=1, keepdims=True)
        weights = [jnp.exp(score - cache_peak) for score in scores]
        summed = weights[0]
        for weight in weights[1:]:
            summed = summed + weight
        cache_total = jnp.sum(summed, axis=1, keepdims=True)
        following = at + 1 < len(items)
        if following:
            current = ready(items[at + 1], extras[at + 1])
        scores = []
        full = [None] * pairs
        for j in range(blocks):
            if following:
                scores.append(score_block(*current, j))
            values = block_of(1, places, j)
            rounded = weights[j].astype(bf16)
            for i in range(pairs):
                part = jnp.dot(
                    rounded[i * rows : (i + 1) * rows],
                    values[:, i * pair_width : (i + 1) * pair_width],
                    preferred_element_type=f32,
                )
                full[i] = part if full[i] is None else full[i] + part
        gathered = jnp.concatenate(
            [
                full[k // 2][(k % 2) * group : (k % 2 + 1) * group, (k % 2) * HD : (k % 2 + 1) * HD]
                for k in range(kv_heads)
            ],
            axis=0,
        )
        own = extra[:, extra.shape[1] - HD :].astype(f32)
        own_keys = jnp.concatenate(
            [jnp.broadcast_to(own[k : k + 1], (group, HD)) for k in range(kv_heads)], axis=0
        )
        own_values = jnp.concatenate(
            [jnp.broadcast_to(own[kv_heads + k : kv_heads + k + 1], (group, HD)) for k in range(kv_heads)],
            axis=0,
        )
        head_rows = jnp.concatenate(halves_of(extra), axis=0).astype(f32)
        own_score = jnp.sum(head_rows * own_keys, axis=1, keepdims=True) * scale
        joint_peak = jnp.maximum(cache_peak, own_score)
        cache_weight = jnp.exp(cache_peak - joint_peak)
        own_weight = jnp.exp(own_score - joint_peak)
        numerator = cache_weight * gathered + own_weight * own_values
        attended = numerator / (cache_weight * cache_total + own_weight)
        out(attended)


def rates_kernel(plan, conv, dt, a_log, bias, skip, later, rate, step_rows, drive_rows, direct):
    for entry in range(24):
        later[entry] = plan[entry]
    mixer = conv[...].astype(f32)
    step_in = dt[...].astype(f32) + bias[...]
    step = jnp.maximum(step_in, 0.0) + jnp.log1p(jnp.exp(-jnp.abs(step_in)))
    drive = step * mixer
    direct[...] = skip[...] * mixer
    for row in range(SLOTS):
        step_rows[row] = step[row : row + 1]
        drive_rows[row] = drive[row : row + 1]
    rate[...] = jnp.exp(a_log[...]) * (-LOG2E)


def rates(plan, conv, dt, a_log, bias, skip):
    slots, width = conv.shape
    rows = pltpu.VMEM((slots, 1, width), f32)
    return pl.pallas_call(
        rates_kernel,
        out_shape=(pltpu.SMEM(plan.shape, jnp.int32), pltpu.VMEM(a_log.shape, f32), rows, rows, pltpu.VMEM((slots, width), f32)),
        in_specs=[whole(pltpu.SMEM)] + [whole(pltpu.VMEM)] * 5,
        out_specs=(whole(pltpu.SMEM),) + (whole(pltpu.VMEM),) * 4,
        compiler_params=pltpu.CompilerParams(vmem_limit_bytes=8 * 2**20),
        cost_estimate=pl.CostEstimate(
            flops=10 * slots * width,
            transcendentals=a_log.size + 2 * slots * width,
            bytes_accessed=a_log.size * 4,
        ),
    )(plan, conv, dt, a_log, bias, skip)


def update_items(
    items, plan, gains, rate, step_rows, drive_rows, held, moved, new_state, mixed_rows, out_buf, sems
):
    n, width = rate.shape
    coupled = gains[...]
    lane = lax.broadcasted_iota(jnp.int32, coupled.shape, 1)
    copies = []
    for i, item in enumerate(items):
        slot = plan[8 + item]
        column = jnp.sum(jnp.where(lane == slot, coupled, 0.0), axis=1, keepdims=True)
        input_gain = jnp.broadcast_to(column[0:n], (n, HD))
        read_gain = jnp.broadcast_to(column[n : 2 * n], (n, HD))
        for c in range(0, width, HD):
            at = slice(c, c + HD)
            previous = held[plan[BITS], :, at] if item == BITS else moved[i][:, at].astype(f32)
            step_row = jnp.broadcast_to(step_rows[slot, :, at], (n, HD))
            drive_row = jnp.broadcast_to(drive_rows[slot, :, at], (n, HD))
            updated = jnp.exp2(step_row * rate[:, at]) * previous + drive_row * input_gain
            out_buf[i, :, at] = updated
            mixed_rows[slot, :, at] = jnp.sum(read_gain * updated, axis=0, keepdims=True)
        copies.append(pltpu.make_async_copy(out_buf.at[i], new_state.at[slot], sems.at[i]))
        copies[-1].start()
    return copies


def first_kernel(
    plan, table, pool, held, heads, q0, q1, gains, gains_far, later, coupled, own, row0, row1
):
    width = held.shape[-1]
    coupled[...] = gains[...] + gains_far[...]
    for entry in range(24):
        later[entry] = plan[entry]

    def keep(attended):
        own[...] = attended.astype(bf16)

    def into(row):
        def put(attended):
            half = attended.shape[0] // 2
            row[:, width : width + HD] = attended[:half].astype(bf16)
            row[:, width + HD :] = attended[half:].astype(bf16)

        return put

    attend_items(FIRST, plan, table, pool, [heads.at[BITS], q0, q1], [keep, into(row0), into(row1)])
    for bit, row in zip(FAR, (row0, row1)):
        row[:, :width] = held[plan[bit]].astype(bf16)


def attention_cost(count):
    return dict(
        flops=count * 4 * 1280 * 32 * 512,
        transcendentals=count * 1280 * 32,
        bytes_accessed=count * 2 * 80 * 16 * 1024,
    )


def first(plan, table, pool, held, heads, gains, gains_far, queries):
    n, width = held.shape[1:]
    result = pltpu.VMEM((2 * n, HD), bf16)
    return pl.pallas_call(
        first_kernel,
        out_shape=(pltpu.SMEM(plan.shape, jnp.int32), pltpu.VMEM(gains.shape, f32), result)
        + (pltpu.VMEM((n, width + 2 * HD), bf16),) * len(FAR),
        in_specs=[whole(pltpu.SMEM)] * 2 + [whole(pltpu.VMEM)] * (5 + len(FAR)),
        out_specs=(whole(pltpu.SMEM),) + (whole(pltpu.VMEM),) * (2 + len(FAR)),
        compiler_params=pltpu.CompilerParams(vmem_limit_bytes=8 * 2**20),
        cost_estimate=pl.CostEstimate(**attention_cost(len(FIRST))),
    )(plan, table, *in_vmem(pool, held, heads, *queries, gains, gains_far))


def near_kernel(plan, table, pool, x0, x1, x2, later, a0, a1, a2):
    for entry in range(24):
        later[entry] = plan[entry]

    def into(out):
        def put(attended):
            out[...] = attended.astype(bf16)

        return put

    attend_items(NEAR, plan, table, pool, [x0, x1, x2], [into(a0), into(a1), into(a2)])


def near(plan, table, pool, extras):
    result = pltpu.VMEM((2 * extras[0].shape[0], HD), bf16)
    return pl.pallas_call(
        near_kernel,
        out_shape=(pltpu.SMEM(plan.shape, jnp.int32),) + (result,) * len(NEAR),
        in_specs=[whole(pltpu.SMEM)] * 2 + [whole(pltpu.VMEM)] * (1 + len(NEAR)),
        out_specs=(whole(pltpu.SMEM),) + (whole(pltpu.VMEM),) * len(NEAR),
        compiler_params=pltpu.CompilerParams(vmem_limit_bytes=8 * 2**20),
        cost_estimate=pl.CostEstimate(**attention_cost(len(NEAR))),
    )(plan, table, *in_vmem(pool, *extras))


def last_kernel(
    plan, gains, rate, step_rows, drive_rows, direct, own, held, x0, x1, x2, x3, x4, b0, b1, b2,
    new_state, final, placed,
    mixed_rows, mixed_all, out_buf, sems,
):
    slots, width = direct.shape
    copies = update_items(
        (BITS,) + NEAR + FAR, plan, gains, rate, step_rows, drive_rows, held, [None, x0, x1, x2, x3, x4],
        new_state, mixed_rows, out_buf, sems,
    )
    mixed_all[...] = jnp.zeros_like(mixed_all)
    for slot in range(slots):
        mixed_all[slot : slot + 1, :] = mixed_rows[slot] + direct[slot : slot + 1, :]
    final[:, :width] = mixed_all[...].astype(bf16)
    results = [own[...].astype(f32)]
    for row in (x3, x4):
        results.append(
            jnp.concatenate([row[:, width : width + HD], row[:, width + HD :]], axis=0).astype(f32)
        )
    for i, result in enumerate(results):
        for k in range(result.shape[0] // 8):
            start = width + (4 * i + k) * HD
            final[:, start : start + HD] = result[8 * k : 8 * k + 8].astype(bf16)
    for item, back in zip(NEAR, (b0, b1, b2)):
        placed[plan[8 + item]] = back[...].astype(f32)
    for copy in copies:
        copy.wait()


def last(plan, gains, made, own, held, extras, backs):
    slots, n, width = held.shape
    inputs = in_vmem(gains, *made, own, held, *extras, *backs)
    vmem = whole(pltpu.VMEM)
    return pl.pallas_call(
        last_kernel,
        out_shape=(
            pltpu.HBM(held.shape, f32),
            pltpu.VMEM((8, width + 12 * HD), bf16),
            pltpu.VMEM((slots, 2 * n, HD), f32),
        ),
        in_specs=[whole(pltpu.SMEM)] + [vmem] * len(inputs),
        out_specs=(whole(pl.ANY), vmem, vmem),
        scratch_shapes=[
            pltpu.VMEM((slots, 1, width), f32),
            pltpu.VMEM((8, width), f32),
            pltpu.VMEM((slots, n, width), f32),
            pltpu.SemaphoreType.DMA((slots,)),
        ],
        compiler_params=pltpu.CompilerParams(vmem_limit_bytes=8 * 2**20),
        cost_estimate=pl.CostEstimate(
            flops=8 * held.size, transcendentals=held.size, bytes_accessed=6 * held.size
        ),
    )(plan, *inputs)


def place_kernel(plan, final, placed, attended, handed, head_rows, rows, rounded, mixed, sems):
    slots, width = mixed.shape
    mixed[...] = final[:, :width][0:slots]
    through = pltpu.make_async_copy(mixed, handed, sems.at[0])
    through.start()
    head_rows[...] = placed[...]
    for i, item in enumerate(FIRST):
        for k in range(head_rows.shape[1] // 8):
            start = width + (4 * i + k) * HD
            head_rows[plan[8 + item], 8 * k : 8 * k + 8] = final[:, start : start + HD].astype(f32)
    for slot in range(slots):
        for h in range(head_rows.shape[1]):
            rows[slot : slot + 1, h * HD : (h + 1) * HD] = head_rows[slot, h : h + 1, :]
    rounded[...] = rows[...].astype(bf16)
    out = pltpu.make_async_copy(rounded, attended, sems.at[1])
    out.start()
    through.wait()
    out.wait()


def place(plan, final, placed):
    heads = placed.shape[1]
    shape = (SLOTS, heads * HD)
    mixed = (SLOTS, final.shape[1] - 12 * HD)
    return pl.pallas_call(
        place_kernel,
        out_shape=(pltpu.HBM(shape, bf16), pltpu.HBM(mixed, bf16)),
        in_specs=[whole(pltpu.SMEM)] + [whole(pltpu.VMEM)] * 2,
        out_specs=(whole(pl.ANY),) * 2,
        scratch_shapes=[
            pltpu.VMEM((SLOTS, heads, HD), f32),
            pltpu.VMEM(shape, f32),
            pltpu.VMEM(shape, bf16),
            pltpu.VMEM(mixed, bf16),
            pltpu.SemaphoreType.DMA((2,)),
        ],
    )(plan, *in_vmem(final, placed))


def per_device(
    source_slot,
    lengths,
    block_table,
    queries,
    kv_pool,
    new_kv,
    ssm_state,
    conv_out,
    dt_raw,
    x_proj,
    a_log,
    dt_bias,
    skip_gain,
):
    fresh = jnp.transpose(new_kv[0], (1, 0, 2))
    held = ssm_state[0]
    pool = kv_pool[0]
    plan, table, gains, heads, *queries_far = load(
        source_slot, lengths, block_table, queries[0], fresh, conv_out[0], x_proj[0]
    )
    gains_far = swapped(gains, "tensor", 0)
    queries_far = [swapped(value, "replica", bit) for bit, value in zip(FAR, queries_far)]
    plan, *rows = pack(plan, held, heads)
    rows_near = [swapped(value, "replica", bit) for bit, value in zip(NEAR, rows)]
    plan, gains, own, *rows = first(plan, table, pool, held, heads, gains, gains_far, queries_far)
    rows_far = [swapped(value, "replica", bit) for bit, value in zip(FAR, rows)]
    plan, *made = rates(plan, conv_out[0], dt_raw[0], a_log[0], dt_bias, skip_gain)
    plan, *attended = near(plan, table, pool, rows_near)
    backs = [across(value, bit) for bit, value in zip(NEAR, attended)]
    new_state, final, placed = last(plan, gains, made, own, held, rows_near + rows_far, backs)
    handed_attention, handed_mamba = place(plan, across(final, BITS), placed)
    return handed_mamba[None], handed_attention[None], new_state[None]


def solution(mesh):
    in_specs = (
        P(),
        P(),
        P("replica", None),
        P("section", "replica", "tensor"),
        P("section", None, "replica", None, "tensor"),
        P("section", None, "replica", "tensor"),
        P("section", "replica", None, "tensor"),
        P("section", "replica", "tensor"),
        P("section", "replica", "tensor"),
        P("section", None, "tensor"),
        P("section", None, "tensor"),
        P("section", "tensor"),
        P("section", "tensor"),
    )
    out_specs = (
        P("section", "replica", "tensor"),
        P("section", "replica", "tensor"),
        P("section", "replica", None, "tensor"),
    )
    return jax.shard_map(
        per_device, mesh=mesh, in_specs=in_specs, out_specs=out_specs, check_vma=False
    )
```

```python
import jax
import jax.numpy as jnp
from jax import lax
from jax.experimental import pallas as pl
from jax.experimental.pallas import tpu as pltpu
from jax.sharding import PartitionSpec as P

HEADS = 64
KVH = 8
HD = 128

SLOTS = 6
BITS = 5
FAR = (2, 4)
NEAR = (1, 3, 0)
FIRST = (BITS,) + FAR
BLOCK = 640
LOG2E = 1.4426950408889634
WEIGHT = 10**10

masked_score = -1e30
f32 = jnp.float32
bf16 = jnp.bfloat16


def swapped(value, axis, bit):
    mask = 2**bit
    pairs = [(source, source ^ mask) for source in range(lax.axis_size(axis))]
    return lax.ppermute(value, axis, pairs)


def across(value, bit):
    sections, replicas = lax.axis_size("section"), lax.axis_size("replica")
    mask = 2**bit if bit < BITS else 0
    pairs = [
        (s * replicas + r, ((s + 1) % sections) * replicas + (r ^ mask))
        for s in range(sections)
        for r in range(replicas)
    ]
    return lax.ppermute(value, ("section", "replica"), pairs)


def whole(space):
    return pl.BlockSpec(memory_space=space)


def in_hbm(*values):
    return [pltpu.with_memory_space_constraint(value, pltpu.HBM) for value in values]


def in_vmem(*values):
    return [pltpu.with_memory_space_constraint(value, pltpu.VMEM) for value in values]


def write_plan(own, src, lens, plan):
    first = own * SLOTS
    for entry in range(24):
        plan[entry] = 0
    for bit in range(BITS):
        partner = jnp.bitwise_xor(own, 1 << bit) * SLOTS
        leave = jnp.int32(0)
        served = jnp.int32(1)
        ask = jnp.int32(0)
        for j in range(SLOTS):
            there = src[partner + j] - first
            gives = (there >= 0) & (there < SLOTS)
            leave = jnp.where(gives, there, leave)
            served = jnp.where(gives, lens[partner + j], served)
            here = src[first + j] - partner
            ask = jnp.where((here >= 0) & (here < SLOTS), j, ask)
        plan[bit] = leave
        plan[8 + bit] = ask
        plan[16 + bit] = served
    kept_old = jnp.int32(0)
    kept_new = jnp.int32(0)
    for j in range(SLOTS):
        here = src[first + j] - first
        stays = (here >= 0) & (here < SLOTS)
        kept_old = jnp.where(stays, here, kept_old)
        kept_new = jnp.where(stays, j, kept_new)
    plan[5] = kept_old
    plan[13] = kept_new
    plan[21] = lens[first + kept_new]


def load_kernel(
    src_in, lens_in, table_in, queries, fresh, conv, x_proj, plan, table, gains, heads_out, far0, far1,
    src, lens, q_buf, fresh_buf, conv_buf, x_buf, head_rows, own_rows, sems,
):
    copies = [
        pltpu.make_async_copy(source, target, sems.at[i])
        for i, (source, target) in enumerate(
            (
                (src_in, src), (lens_in, lens), (queries, q_buf), (fresh, fresh_buf),
                (table_in, table), (conv, conv_buf), (x_proj, x_buf),
            )
        )
    ]
    for copy in copies:
        copy.start()
    copies[0].wait()
    copies[1].wait()
    write_plan(lax.axis_index("replica"), src, lens, plan)
    copies[2].wait()
    copies[3].wait()
    heads = head_rows.shape[1]
    half = heads // 2
    keys = fresh_buf.shape[-1] // HD
    own_rows[...] = jnp.zeros_like(own_rows)
    for h in range(heads):
        column = q_buf[:, h * HD : (h + 1) * HD].astype(f32)
        for slot in range(SLOTS):
            head_rows[slot, h : h + 1, :] = column[slot : slot + 1]
    for item in range(BITS + 1):
        slot = plan[8 + item]
        pair = fresh_buf[slot].astype(f32)
        for k in range(keys):
            own_rows[k : k + 1, :] = pair[0:1, k * HD : (k + 1) * HD]
            own_rows[keys + k : keys + k + 1, :] = pair[1:2, k * HD : (k + 1) * HD]
        heads_out[item] = jnp.concatenate(
            [head_rows[slot, 0:half], head_rows[slot, half:heads], own_rows[...]], axis=1
        ).astype(bf16)
    for bit, out in zip(FAR, (far0, far1)):
        out[...] = heads_out[bit]
    copies[4].wait()
    copies[5].wait()
    copies[6].wait()
    gains[...] = lax.dot_general(
        x_buf[...], conv_buf[...], (((1,), (1,)), ((), ())), preferred_element_type=f32
    )


def load(source_slot, lengths, block_table, queries, fresh, conv, x_proj):
    heads = queries.shape[1] // HD
    half = heads // 2
    return pl.pallas_call(
        load_kernel,
        out_shape=(
            pltpu.SMEM((24,), jnp.int32),
            pltpu.SMEM(block_table.shape, jnp.int32),
            pltpu.VMEM((x_proj.shape[0], SLOTS), f32),
            pltpu.VMEM((BITS + 1, half, 3 * HD), bf16),
        )
        + (pltpu.VMEM((half, 3 * HD), bf16),) * len(FAR),
        in_specs=[whole(pl.ANY)] * 7,
        out_specs=(whole(pltpu.SMEM),) * 2 + (whole(pltpu.VMEM),) * (2 + len(FAR)),
        scratch_shapes=[
            pltpu.SMEM(source_slot.shape, jnp.int32),
            pltpu.SMEM(lengths.shape, jnp.int32),
            pltpu.VMEM(queries.shape, bf16),
            pltpu.VMEM(fresh.shape, bf16),
            pltpu.VMEM(conv.shape, bf16),
            pltpu.VMEM(x_proj.shape, bf16),
            pltpu.VMEM((SLOTS, heads, HD), f32),
            pltpu.VMEM((half, HD), f32),
            pltpu.SemaphoreType.DMA((7,)),
        ],
        compiler_params=pltpu.CompilerParams(vmem_limit_bytes=4 * 2**20),
        cost_estimate=pl.CostEstimate(flops=WEIGHT, transcendentals=0, bytes_accessed=queries.size * 2),
    )(*in_hbm(source_slot, lengths, block_table, queries, fresh, conv, x_proj))


def pack_kernel(plan, held, heads, later, *packs):
    width = held.shape[-1]
    for entry in range(24):
        later[entry] = plan[entry]
    for bit, out in zip(NEAR, packs):
        out[:, :width] = held[plan[bit]].astype(bf16)
        out[:, width:] = heads[bit]


def pack(plan, held, heads):
    n, width = held.shape[1:]
    return pl.pallas_call(
        pack_kernel,
        out_shape=(pltpu.SMEM(plan.shape, jnp.int32),)
        + (pltpu.VMEM((n, width + heads.shape[-1]), bf16),) * len(NEAR),
        in_specs=[whole(pltpu.SMEM)] + [whole(pltpu.VMEM)] * 2,
        out_specs=(whole(pltpu.SMEM),) + (whole(pltpu.VMEM),) * len(NEAR),
        compiler_params=pltpu.CompilerParams(vmem_limit_bytes=4 * 2**20),
        cost_estimate=pl.CostEstimate(
            flops=0, transcendentals=0, bytes_accessed=held.size * 3
        ),
    )(plan, *in_vmem(held, heads))


def attend_items(items, plan, table, pool, extras, outs):
    page = pool.shape[2]
    pages = table.shape[1]
    per_block = BLOCK // page
    blocks = pages // per_block
    pair_width = 2 * HD
    pairs = pool.shape[3] // pair_width
    group = HEADS // KVH
    rows = 2 * group
    kv_heads = 2 * pairs
    scale = HD ** (-0.5)
    row_id = lax.broadcasted_iota(jnp.int32, (rows, pair_width), 0)
    lane_id = lax.broadcasted_iota(jnp.int32, (rows, pair_width), 1)
    own_block = (row_id < group) == (lane_id < HD)
    token_id = lax.broadcasted_iota(jnp.int32, (rows * pairs, BLOCK), 1)

    def block_of(which, places, j):
        return jnp.concatenate(
            [pool[which, places[j * per_block + u]] for u in range(per_block)], axis=0
        )

    def places_of(item):
        slot = plan[item]
        return [table[slot, p] for p in range(pages)]

    def halves_of(extra):
        base = extra.shape[1] - 3 * HD
        return [extra[:, base + i * HD : base + (i + 1) * HD] for i in range(2)]

    def score_block(spread, length, places, j):
        keys = block_of(0, places, j)
        parts = [
            lax.dot_general(
                spread[i],
                keys[:, i * pair_width : (i + 1) * pair_width],
                (((1,), (1,)), ((), ())),
                preferred_element_type=f32,
            )
            for i in range(pairs)
        ]
        score = jnp.concatenate(parts, axis=0) * scale
        return jnp.where(token_id < length - j * BLOCK, score, masked_score)

    def ready(item, extra):
        spread = [
            jnp.where(own_block, jnp.concatenate([half, half], axis=1).astype(f32), 0.0).astype(bf16)
            for half in halves_of(extra)
        ]
        return spread, plan[16 + item], places_of(item)

    current = ready(items[0], extras[0])
    scores = [score_block(*current, j) for j in range(blocks)]
    for at, (extra, out) in enumerate(zip(extras, outs)):
        places = current[2]
        top = scores[0]
        for score in scores[1:]:
            top = jnp.maximum(top, score)
        cache_peak = jnp.max(top, axis=1, keepdims=True)
        weights = [jnp.exp(score - cache_peak) for score in scores]
        summed = weights[0]
        for weight in weights[1:]:
            summed = summed + weight
        cache_total = jnp.sum(summed, axis=1, keepdims=True)
        following = at + 1 < len(items)
        if following:
            current = ready(items[at + 1], extras[at + 1])
        scores = []
        full = [None] * pairs
        for j in range(blocks):
            if following:
                scores.append(score_block(*current, j))
            values = block_of(1, places, j)
            rounded = weights[j].astype(bf16)
            for i in range(pairs):
                part = jnp.dot(
                    rounded[i * rows : (i + 1) * rows],
                    values[:, i * pair_width : (i + 1) * pair_width],
                    preferred_element_type=f32,
                )
                full[i] = part if full[i] is None else full[i] + part
        gathered = jnp.concatenate(
            [
                full[k // 2][(k % 2) * group : (k % 2 + 1) * group, (k % 2) * HD : (k % 2 + 1) * HD]
                for k in range(kv_heads)
            ],
            axis=0,
        )
        own = extra[:, extra.shape[1] - HD :].astype(f32)
        own_keys = jnp.concatenate(
            [jnp.broadcast_to(own[k : k + 1], (group, HD)) for k in range(kv_heads)], axis=0
        )
        own_values = jnp.concatenate(
            [jnp.broadcast_to(own[kv_heads + k : kv_heads + k + 1], (group, HD)) for k in range(kv_heads)],
            axis=0,
        )
        head_rows = jnp.concatenate(halves_of(extra), axis=0).astype(f32)
        own_score = jnp.sum(head_rows * own_keys, axis=1, keepdims=True) * scale
        joint_peak = jnp.maximum(cache_peak, own_score)
        cache_weight = jnp.exp(cache_peak - joint_peak)
        own_weight = jnp.exp(own_score - joint_peak)
        numerator = cache_weight * gathered + own_weight * own_values
        attended = numerator / (cache_weight * cache_total + own_weight)
        out(attended)


def rates_kernel(plan, conv, dt, a_log, bias, skip, later, rate, step_rows, drive_rows, direct):
    for entry in range(24):
        later[entry] = plan[entry]
    mixer = conv[...].astype(f32)
    step_in = dt[...].astype(f32) + bias[...]
    step = jnp.maximum(step_in, 0.0) + jnp.log1p(jnp.exp(-jnp.abs(step_in)))
    drive = step * mixer
    direct[...] = skip[...] * mixer
    for row in range(SLOTS):
        step_rows[row] = step[row : row + 1]
        drive_rows[row] = drive[row : row + 1]
    rate[...] = jnp.exp(a_log[...]) * (-LOG2E)


def rates(plan, conv, dt, a_log, bias, skip):
    slots, width = conv.shape
    rows = pltpu.VMEM((slots, 1, width), f32)
    return pl.pallas_call(
        rates_kernel,
        out_shape=(pltpu.SMEM(plan.shape, jnp.int32), pltpu.VMEM(a_log.shape, f32), rows, rows, pltpu.VMEM((slots, width), f32)),
        in_specs=[whole(pltpu.SMEM)] + [whole(pltpu.VMEM)] * 5,
        out_specs=(whole(pltpu.SMEM),) + (whole(pltpu.VMEM),) * 4,
        compiler_params=pltpu.CompilerParams(vmem_limit_bytes=8 * 2**20),
        cost_estimate=pl.CostEstimate(
            flops=10 * slots * width,
            transcendentals=a_log.size + 2 * slots * width,
            bytes_accessed=a_log.size * 4,
        ),
    )(plan, conv, dt, a_log, bias, skip)


def update_items(
    items, plan, gains, rate, step_rows, drive_rows, held, moved, new_state, mixed_rows, out_buf, sems
):
    n, width = rate.shape
    coupled = gains[...]
    lane = lax.broadcasted_iota(jnp.int32, coupled.shape, 1)
    copies = []
    for i, item in enumerate(items):
        slot = plan[8 + item]
        column = jnp.sum(jnp.where(lane == slot, coupled, 0.0), axis=1, keepdims=True)
        input_gain = jnp.broadcast_to(column[0:n], (n, HD))
        read_gain = jnp.broadcast_to(column[n : 2 * n], (n, HD))
        for c in range(0, width, HD):
            at = slice(c, c + HD)
            previous = held[plan[BITS], :, at] if item == BITS else moved[i][:, at].astype(f32)
            step_row = jnp.broadcast_to(step_rows[slot, :, at], (n, HD))
            drive_row = jnp.broadcast_to(drive_rows[slot, :, at], (n, HD))
            updated = jnp.exp2(step_row * rate[:, at]) * previous + drive_row * input_gain
            out_buf[i, :, at] = updated
            mixed_rows[slot, :, at] = jnp.sum(read_gain * updated, axis=0, keepdims=True)
        copies.append(pltpu.make_async_copy(out_buf.at[i], new_state.at[slot], sems.at[i]))
        copies[-1].start()
    return copies


def first_kernel(
    plan, table, pool, held, heads, q0, q1, gains, gains_far, later, coupled, own, row0, row1
):
    width = held.shape[-1]
    coupled[...] = gains[...] + gains_far[...]
    for entry in range(24):
        later[entry] = plan[entry]

    def keep(attended):
        own[...] = attended.astype(bf16)

    def into(row):
        def put(attended):
            half = attended.shape[0] // 2
            row[:, width : width + HD] = attended[:half].astype(bf16)
            row[:, width + HD :] = attended[half:].astype(bf16)

        return put

    attend_items(FIRST, plan, table, pool, [heads.at[BITS], q0, q1], [keep, into(row0), into(row1)])
    for bit, row in zip(FAR, (row0, row1)):
        row[:, :width] = held[plan[bit]].astype(bf16)


def attention_cost(count):
    return dict(
        flops=count * 4 * 1280 * 32 * 512,
        transcendentals=count * 1280 * 32,
        bytes_accessed=count * 2 * 80 * 16 * 1024,
    )


def first(plan, table, pool, held, heads, gains, gains_far, queries):
    n, width = held.shape[1:]
    result = pltpu.VMEM((2 * n, HD), bf16)
    return pl.pallas_call(
        first_kernel,
        out_shape=(pltpu.SMEM(plan.shape, jnp.int32), pltpu.VMEM(gains.shape, f32), result)
        + (pltpu.VMEM((n, width + 2 * HD), bf16),) * len(FAR),
        in_specs=[whole(pltpu.SMEM)] * 2 + [whole(pltpu.VMEM)] * (5 + len(FAR)),
        out_specs=(whole(pltpu.SMEM),) + (whole(pltpu.VMEM),) * (2 + len(FAR)),
        compiler_params=pltpu.CompilerParams(vmem_limit_bytes=8 * 2**20),
        cost_estimate=pl.CostEstimate(**attention_cost(len(FIRST))),
    )(plan, table, *in_vmem(pool, held, heads, *queries, gains, gains_far))


def near_kernel(plan, table, pool, x0, x1, x2, later, a0, a1, a2):
    for entry in range(24):
        later[entry] = plan[entry]

    def into(out):
        def put(attended):
            out[...] = attended.astype(bf16)

        return put

    attend_items(NEAR, plan, table, pool, [x0, x1, x2], [into(a0), into(a1), into(a2)])


def near(plan, table, pool, extras):
    result = pltpu.VMEM((2 * extras[0].shape[0], HD), bf16)
    return pl.pallas_call(
        near_kernel,
        out_shape=(pltpu.SMEM(plan.shape, jnp.int32),) + (result,) * len(NEAR),
        in_specs=[whole(pltpu.SMEM)] * 2 + [whole(pltpu.VMEM)] * (1 + len(NEAR)),
        out_specs=(whole(pltpu.SMEM),) + (whole(pltpu.VMEM),) * len(NEAR),
        compiler_params=pltpu.CompilerParams(vmem_limit_bytes=8 * 2**20),
        cost_estimate=pl.CostEstimate(**attention_cost(len(NEAR))),
    )(plan, table, *in_vmem(pool, *extras))


def last_kernel(
    plan, gains, rate, step_rows, drive_rows, direct, own, held, x0, x1, x2, x3, x4, b0, b1, b2,
    new_state, final, placed,
    mixed_rows, mixed_all, out_buf, sems,
):
    slots, width = direct.shape
    copies = update_items(
        (BITS,) + NEAR + FAR, plan, gains, rate, step_rows, drive_rows, held, [None, x0, x1, x2, x3, x4],
        new_state, mixed_rows, out_buf, sems,
    )
    mixed_all[...] = jnp.zeros_like(mixed_all)
    for slot in range(slots):
        mixed_all[slot : slot + 1, :] = mixed_rows[slot] + direct[slot : slot + 1, :]
    final[:, :width] = mixed_all[...].astype(bf16)
    results = [own[...].astype(f32)]
    for row in (x3, x4):
        results.append(
            jnp.concatenate([row[:, width : width + HD], row[:, width + HD :]], axis=0).astype(f32)
        )
    for i, result in enumerate(results):
        for k in range(result.shape[0] // 8):
            start = width + (4 * i + k) * HD
            final[:, start : start + HD] = result[8 * k : 8 * k + 8].astype(bf16)
    for item, back in zip(NEAR, (b0, b1, b2)):
        placed[plan[8 + item]] = back[...].astype(f32)
    for copy in copies:
        copy.wait()


def last(plan, gains, made, own, held, extras, backs):
    slots, n, width = held.shape
    inputs = in_vmem(gains, *made, own, held, *extras, *backs)
    vmem = whole(pltpu.VMEM)
    return pl.pallas_call(
        last_kernel,
        out_shape=(
            pltpu.HBM(held.shape, f32),
            pltpu.VMEM((8, width + 12 * HD), bf16),
            pltpu.VMEM((slots, 2 * n, HD), f32),
        ),
        in_specs=[whole(pltpu.SMEM)] + [vmem] * len(inputs),
        out_specs=(whole(pl.ANY), vmem, vmem),
        scratch_shapes=[
            pltpu.VMEM((slots, 1, width), f32),
            pltpu.VMEM((8, width), f32),
            pltpu.VMEM((slots, n, width), f32),
            pltpu.SemaphoreType.DMA((slots,)),
        ],
        compiler_params=pltpu.CompilerParams(vmem_limit_bytes=8 * 2**20),
        cost_estimate=pl.CostEstimate(
            flops=8 * held.size, transcendentals=held.size, bytes_accessed=6 * held.size
        ),
    )(plan, *inputs)


def place_kernel(plan, final, placed, attended, handed, head_rows, rows, rounded, mixed, sems):
    slots, width = mixed.shape
    mixed[...] = final[:, :width][0:slots]
    through = pltpu.make_async_copy(mixed, handed, sems.at[0])
    through.start()
    head_rows[...] = placed[...]
    for i, item in enumerate(FIRST):
        for k in range(head_rows.shape[1] // 8):
            start = width + (4 * i + k) * HD
            head_rows[plan[8 + item], 8 * k : 8 * k + 8] = final[:, start : start + HD].astype(f32)
    for slot in range(slots):
        for h in range(head_rows.shape[1]):
            rows[slot : slot + 1, h * HD : (h + 1) * HD] = head_rows[slot, h : h + 1, :]
    rounded[...] = rows[...].astype(bf16)
    out = pltpu.make_async_copy(rounded, attended, sems.at[1])
    out.start()
    through.wait()
    out.wait()


def place(plan, final, placed):
    heads = placed.shape[1]
    shape = (SLOTS, heads * HD)
    mixed = (SLOTS, final.shape[1] - 12 * HD)
    return pl.pallas_call(
        place_kernel,
        out_shape=(pltpu.HBM(shape, bf16), pltpu.HBM(mixed, bf16)),
        in_specs=[whole(pltpu.SMEM)] + [whole(pltpu.VMEM)] * 2,
        out_specs=(whole(pl.ANY),) * 2,
        scratch_shapes=[
            pltpu.VMEM((SLOTS, heads, HD), f32),
            pltpu.VMEM(shape, f32),
            pltpu.VMEM(shape, bf16),
            pltpu.VMEM(mixed, bf16),
            pltpu.SemaphoreType.DMA((2,)),
        ],
    )(plan, *in_vmem(final, placed))


def per_device(
    source_slot,
    lengths,
    block_table,
    queries,
    kv_pool,
    new_kv,
    ssm_state,
    conv_out,
    dt_raw,
    x_proj,
    a_log,
    dt_bias,
    skip_gain,
):
    fresh = jnp.transpose(new_kv[0], (1, 0, 2))
    held = ssm_state[0]
    pool = kv_pool[0]
    plan, table, gains, heads, *queries_far = load(
        source_slot, lengths, block_table, queries[0], fresh, conv_out[0], x_proj[0]
    )
    gains_far = swapped(gains, "tensor", 0)
    queries_far = [swapped(value, "replica", bit) for bit, value in zip(FAR, queries_far)]
    plan, *rows = pack(plan, held, heads)
    rows_near = [swapped(value, "replica", bit) for bit, value in zip(NEAR, rows)]
    plan, gains, own, *rows = first(plan, table, pool, held, heads, gains, gains_far, queries_far)
    rows_far = [swapped(value, "replica", bit) for bit, value in zip(FAR, rows)]
    plan, *made = rates(plan, conv_out[0], dt_raw[0], a_log[0], dt_bias, skip_gain)
    plan, *attended = near(plan, table, pool, rows_near)
    backs = [across(value, bit) for bit, value in zip(NEAR, attended)]
    new_state, final, placed = last(plan, gains, made, own, held, rows_near + rows_far, backs)
    handed_attention, handed_mamba = place(plan, across(final, BITS), placed)
    return handed_mamba[None], handed_attention[None], new_state[None]


def solution(mesh):
    in_specs = (
        P(),
        P(),
        P("replica", None),
        P("section", "replica", "tensor"),
        P("section", None, "replica", None, "tensor"),
        P("section", None, "replica", "tensor"),
        P("section", "replica", None, "tensor"),
        P("section", "replica", "tensor"),
        P("section", "replica", "tensor"),
        P("section", None, "tensor"),
        P("section", None, "tensor"),
        P("section", "tensor"),
        P("section", "tensor"),
    )
    out_specs = (
        P("section", "replica", "tensor"),
        P("section", "replica", "tensor"),
        P("section", "replica", None, "tensor"),
    )
    return jax.shard_map(
        per_device, mesh=mesh, in_specs=in_specs, out_specs=out_specs, check_vma=False
    )
```
